32 devices in a mesh: tm: 8 (over z, x), feat: 4 (over y, core).
Axes of the slice: x: 2, y: 2, z: 4, core: 2. Of those that a mesh axis runs over, the one named last changes fastest.
Arguments:
- features: bfloat16 [16384, 512], P('tm'), may hold values from -64 to 64
- seg_lengths: int32 [16], replicated, may hold values from 1 to 4096, 16384 in all
Outputs:
- koopman: float32 [512, 512], P('feat')
- lag_error: float32 [128, 16384], P('feat', 'tm')
The draws below stay inside these ranges and needn't reach their ends.
All inputs are finite; a program needn't handle non-finite values.
Results may differ from the reference program's by a relative error of at most 0.0037.
Values may be sent and summed in bfloat16 or wider, within the bound.
No kernel may reach another device: no remote copies, remote signals or barrier semaphores. Data moves between devices by JAX's collectives and lax.ppermute only.
A program may use at most 64 MiB of HBM per device.

```python
import math
import jax
import jax.numpy as jnp
import numpy as np
from jax import lax

F = 512
LAG = 64
NC = 128
FR_DEV = 2048
FRAMES = 16384
NSEG = 16
SEG_MOST = 4096


def draw_features(key, part):
    key_noise, key_cols, key_rows, key_shift = jax.random.split(key, 4)
    total_rows = FRAMES + LAG
    noise_all = jax.random.normal(key_noise, (total_rows, F), jnp.float32)
    row_scale = jnp.exp(jax.random.uniform(key_rows, (FRAMES, 1), jnp.float32, math.log(0.4), math.log(4.0)))
    recent = noise_all[LAG:]
    mixed_rows = recent + 0.8 * noise_all[:FRAMES] + 0.6 * jnp.roll(recent, 1, axis=1) + 0.45 * jnp.roll(recent, 7, axis=1)
    col_scale = jnp.exp(jax.random.uniform(key_cols, (1, F), jnp.float32, math.log(0.35), math.log(3.5)))
    drift_part = (0.5 + jnp.arange(FRAMES, dtype=jnp.float32)[:, None] / FRAMES) * jax.random.normal(key_shift, (1, F), jnp.float32)
    values = row_scale * col_scale * mixed_rows + drift_part
    return jnp.clip(values, -64.0, 64.0).astype(jnp.bfloat16)


def profile(number_of, total, limit, lean):
    weights = [(1 << 20) // math.isqrt(rank ** lean) + 1 for rank in range(2, number_of + 1)]
    surplus, counts = total - limit - (number_of - 1), [1] * (number_of - 1)
    while surplus > 0:
        free = [i for i in range(number_of - 1) if counts[i] < limit]
        mass, budget = sum([weights[i] for i in free]), surplus
        for i in free:
            more = min(limit - counts[i], max(1, budget * weights[i] // mass), surplus)
            counts[i] = counts[i] + more
            surplus = surplus - more
    return np.array([limit] + counts)


def ragged(stream_key, amount, total, most, slope):
    if amount == 2:
        one = jax.random.randint(stream_key, (), max(1, total - most), min(most, total - 1) + 1)
        return jnp.stack([one, total - one])
    lengths = jnp.asarray(profile(amount, total, most, slope), jnp.int32)
    twos = (amount - 1) // 2
    donor, sink = lengths[1:1 + 2 * twos:2], lengths[2:2 + 2 * twos:2]
    slack = jnp.minimum(donor - 1, most - sink)
    passed = jax.random.randint(jax.random.fold_in(stream_key, 1), (twos,), 0, 1 << 20) % (slack + 1)
    lengths = lengths.at[1:1 + 2 * twos:2].set(donor - passed).at[2:2 + 2 * twos:2].set(sink + passed)
    return lengths[jax.random.permutation(jax.random.fold_in(stream_key, 2), amount)]


def setup_inputs(seed: int = 0) -> dict:
    seeds = jax.random.split(jax.random.key(seed), 3)
    features = draw_features(jax.random.fold_in(seeds[2], 71), 0)
    seg_lengths = ragged(seeds[1], NSEG, FRAMES, SEG_MOST, 2).astype(jnp.int32)
    return {"features": features, "seg_lengths": seg_lengths}


RIDGE = 0.05

def reference(features, seg_lengths):
    frame_count = features.shape[0]
    feat_width = features.shape[1]
    seg_ends = jnp.cumsum(seg_lengths).astype(jnp.int32)
    moments = jnp.arange(frame_count, dtype=jnp.int32)
    later_seg = jnp.searchsorted(seg_ends, moments + LAG, side='right').astype(jnp.int32)
    now_seg = jnp.searchsorted(seg_ends, moments, side='right').astype(jnp.int32)
    validity = (later_seg == now_seg).astype(jnp.float32)
    pair_count = jnp.sum(jnp.maximum(seg_lengths - LAG, 0)).astype(jnp.float32)
    ahead_rows = jnp.concatenate([features[LAG:], jnp.zeros((LAG, feat_width), features.dtype)], axis=0)
    block_count = frame_count // FR_DEV
    highest = lax.Precision.HIGHEST

    def accumulate(totals, pieces):
        lead_rows, later_rows, mask_rows = pieces
        lead_rows = lead_rows.astype(jnp.float32)
        later_rows = later_rows.astype(jnp.float32)
        weights = mask_rows[:, None]
        gram_a = jnp.dot(lead_rows.T, weights * lead_rows, precision=highest) + jnp.dot(later_rows.T, weights * later_rows, precision=highest)
        gram_b = jnp.dot(lead_rows.T, weights * later_rows, precision=highest) + jnp.dot(later_rows.T, weights * lead_rows, precision=highest)
        sum_a = jnp.sum(weights * lead_rows, axis=0)
        sum_b = jnp.sum(weights * later_rows, axis=0)
        return ((totals[0] + gram_a, totals[1] + gram_b, totals[2] + sum_a, totals[3] + sum_b), None)
    square_zero = jnp.zeros((feat_width, feat_width), jnp.float32)
    vector_zero = jnp.zeros((feat_width,), jnp.float32)
    stacked = (features.reshape(block_count, FR_DEV, feat_width), ahead_rows.reshape(block_count, FR_DEV, feat_width), validity.reshape(block_count, FR_DEV))
    (gram_a, gram_b, sum_a, sum_b), _ = lax.scan(accumulate, (square_zero, square_zero, vector_zero, vector_zero), stacked)
    mean_vec = (sum_a + sum_b) / (2.0 * pair_count)
    outer_mean = jnp.outer(mean_vec, mean_vec)
    inst_cov = gram_a / (2.0 * pair_count) - outer_mean
    shifted = inst_cov + RIDGE * (jnp.trace(inst_cov) / feat_width) * jnp.eye(feat_width, dtype=jnp.float32)
    lag_cov = gram_b / (2.0 * pair_count) - outer_mean
    lower_chol = jnp.linalg.cholesky(shifted)
    half_solve = jax.scipy.linalg.solve_triangular(lower_chol, lag_cov, lower=True)
    koopman = jax.scipy.linalg.solve_triangular(lower_chol, half_solve.T, lower=True).T
    unit_basis = jnp.eye(feat_width, dtype=jnp.float32)[:, :NC]
    first_map = jax.scipy.linalg.solve_triangular(lower_chol.T, unit_basis, lower=False).astype(jnp.bfloat16)
    second_map = jax.scipy.linalg.solve_triangular(lower_chol.T, koopman[:, :NC], lower=False).astype(jnp.bfloat16)
    offset = jnp.dot(mean_vec, first_map.astype(jnp.float32) - second_map.astype(jnp.float32), precision=highest)
    lag_resid = jnp.dot(ahead_rows.astype(jnp.float32), first_map.astype(jnp.float32), preferred_element_type=jnp.float32) - jnp.dot(features.astype(jnp.float32), second_map.astype(jnp.float32), preferred_element_type=jnp.float32) - offset[None, :]
    lag_error = (lag_resid * validity[:, None]).T
    return (koopman, lag_error)
```

```python
import functools

import jax
import jax.numpy as jnp
from jax import lax
from jax.experimental import pallas as pl
from jax.experimental.pallas import tpu as pltpu
from jax.sharding import PartitionSpec as P

LAG = 64
NC = 128
RIDGE = 0.05
HIGHEST = lax.Precision.HIGHEST
B = 128
PICKS = 3
F32 = jnp.float32
BF16 = jnp.bfloat16
VMEM_LIMIT = 48 * 2**20


def dot_nn(left, right):
    return jnp.dot(left, right, precision=HIGHEST, preferred_element_type=F32)


def dot_nt(left, right):
    return lax.dot_general(
        left, right, (((1,), (1,)), ((), ())), precision=HIGHEST, preferred_element_type=F32
    )


def contract(left_rows, right_rows):
    return lax.dot_general(
        left_rows, right_rows, (((0,), (0,)), ((), ())), preferred_element_type=F32
    )


def valid_at(seg_ref, moments):
    def step(k, carry):
        end, crossing = carry
        end = end + seg_ref[k]
        hit = (end > moments) & (end <= moments + LAG)
        return end, jnp.where(hit, 1.0, crossing)

    zero = jnp.zeros(moments.shape, F32)
    _, crossing = lax.fori_loop(0, seg_ref.shape[0], step, (jnp.int32(0), zero))
    return 1.0 - crossing


def gram_kernel(chunk_rows, seg_ref, x_ref, halo_ref, out_ref, z_ref):
    frames = x_ref.shape[0]
    feat_count = x_ref.shape[1] // B
    groups = frames // B
    first = lax.axis_index("tm") * frames
    feat = lax.axis_index("feat")
    cols = pl.ds(pl.multiple_of(feat * B, B), B)
    moments = (
        first
        + lax.broadcasted_iota(jnp.int32, (groups, B), 0) * B
        + lax.broadcasted_iota(jnp.int32, (groups, B), 1)
    )
    ahead = valid_at(seg_ref, moments)
    behind = jnp.where(moments >= LAG, valid_at(seg_ref, moments - LAG), 0.0)
    local_behind = jnp.where(moments - first >= LAG, behind, 0.0)
    stacked = jnp.concatenate(
        [ahead, local_behind, ahead + behind, jnp.zeros((B - 3 * groups, B), F32)], axis=0
    )
    columns = stacked.T

    def weight(row):
        return jnp.broadcast_to(columns[:, row : row + 1], (B, B))

    total = jnp.zeros((8, B), F32)
    half = B - LAG
    for g in range(groups):
        low = g * B
        own = x_ref[low : low + B, cols].astype(F32)
        if g + 1 < groups:
            later = x_ref[low + LAG : low + LAG + B, cols].astype(F32)
        else:
            later = jnp.concatenate(
                [x_ref[low + LAG : low + B, cols], halo_ref[:, cols]], axis=0
            ).astype(F32)
        if g > 0:
            earlier = x_ref[low - LAG : low - LAG + B, cols].astype(F32)
        else:
            earlier = jnp.concatenate(
                [x_ref[0:LAG, cols], x_ref[0:half, cols]], axis=0
            ).astype(F32)
        weighted = own * weight(2 * groups + g)
        z_ref[low : low + B, 0:B] = weighted.astype(BF16)
        z_ref[low : low + B, B : 2 * B] = (later * weight(g)).astype(BF16)
        z_ref[low : low + B, 2 * B : 3 * B] = (earlier * weight(groups + g)).astype(BF16)
        for part in range(B // 8):
            total = total + weighted[8 * part : 8 * part + 8]
    tail = x_ref[frames - LAG : frames, cols].astype(F32) * weight(groups - 1)[half:]
    tail = tail.astype(BF16)
    rows = []
    for back in range(PICKS):
        block = lax.rem(feat - back + feat_count, feat_count)
        left = pl.ds(pl.multiple_of(block * B, B), B)
        prod = contract(x_ref[:, left], z_ref[...])
        gram_b = prod[:, B : 2 * B] + prod[:, 2 * B :] + contract(halo_ref[:, left], tail)
        out_ref[back * B : (back + 1) * B, :] = prod[:, :B]
        out_ref[(PICKS + back) * B : (PICKS + back + 1) * B, :] = gram_b
    rows = 2 * PICKS * B
    out_ref[rows : rows + 8, :] = jnp.broadcast_to(jnp.sum(total, axis=0, keepdims=True), (8, B))
    if out_ref.shape[0] > rows + 8:
        out_ref[rows + 8 :, :] = jnp.zeros((out_ref.shape[0] - rows - 8, B), F32)


def across(tile, lane):
    return jnp.broadcast_to(tile[:, lane : lane + 1], tile.shape)


def down(tile, row):
    return jnp.broadcast_to(tile[row : row + 1, :], tile.shape)


def leaf_inverse(square):
    count = square.shape[0] // 8
    lanes = lax.broadcasted_iota(jnp.int32, (8, B), 1)
    sublanes = lax.broadcasted_iota(jnp.int32, (8, B), 0)
    rows = [square[8 * i : 8 * i + 8, :] for i in range(count)]
    extra = [jnp.where(lanes == sublanes + 8 * i, 1.0, 0.0).astype(F32) for i in range(count)]
    result = []
    for b in range(count):
        panel = [across(rows[b], 8 * b + j) for j in range(8)]
        diag = [[down(panel[j], i) if j <= i else None for j in range(8)] for i in range(8)]
        top = [down(rows[b], i) for i in range(8)]
        top_extra = [down(extra[b], i) for i in range(8)]
        below = {k: [across(rows[k], 8 * b + j) for j in range(8)] for k in range(b + 1, count)}
        finished = None
        for i in range(8):
            recip = 1.0 / diag[i][i]
            scale = lax.rsqrt(diag[i][i])
            factor = [None] * 8
            for k in range(i + 1, 8):
                factor[k] = diag[k][i] * recip
            for k in range(i + 1, 8):
                for col in range(i + 1, k + 1):
                    diag[k][col] = diag[k][col] - factor[k] * diag[col][i]
                top[k] = top[k] - factor[k] * top[i]
                top_extra[k] = top_extra[k] - factor[k] * top_extra[i]
            scaled = top_extra[i] * scale
            finished = scaled if finished is None else jnp.where(sublanes == i, scaled, finished)
            for k in range(b + 1, count):
                col_vals = below[k]
                gain = col_vals[i] * recip
                rows[k] = rows[k] - gain * top[i]
                extra[k] = extra[k] - gain * top_extra[i]
                for col in range(i + 1, 8):
                    col_vals[col] = col_vals[col] - gain * diag[col][i]
        result.append(finished)
    return jnp.concatenate(result, axis=0)


def solve_kernel(
    tm_count, seg_ref, sums_ref, x_ref, halo_ref, koop_ref, err_ref, flat_ref, w_ref, b_ref
):
    frames, width = x_ref.shape
    n = width // B
    feat_count = n
    chunk = sums_ref.shape[1]
    first = lax.axis_index("tm") * frames
    feat = lax.axis_index("feat")
    for j in range(tm_count):
        for f in range(feat_count):
            flat_ref[f, j * chunk : (j + 1) * chunk, :] = sums_ref[j * feat_count + f]

    def add_pairs(k, total):
        return total + jnp.maximum(seg_ref[k] - LAG, 0)

    pairs = lax.fori_loop(0, seg_ref.shape[0], add_pairs, jnp.int32(0))
    ones = jnp.ones((8, B), F32)
    inv_pairs = (1.0 / (ones * (2.0 * pairs.astype(F32))))[0:1, :]
    mean_row = [flat_ref[f, 2 * PICKS * B : 2 * PICKS * B + 1, :] * inv_pairs for f in range(n)]
    mean_col = [jnp.broadcast_to(mean_row[f], (B, B)).T for f in range(n)]

    def moment(base, i, j):
        back = (j - i) % n
        if back < PICKS:
            block = flat_ref[j, (base + back) * B : (base + back + 1) * B, :]
        else:
            block = flat_ref[i, (base + n - back) * B : (base + n - back + 1) * B, :].T
        return block * inv_pairs - mean_col[i] * mean_row[j]

    eye = (
        lax.broadcasted_iota(jnp.int32, (B, B), 0) == lax.broadcasted_iota(jnp.int32, (B, B), 1)
    )
    upper = {(i, j): moment(0, i, j) for i in range(n) for j in range(i, n)}
    diag_sum = sum(jnp.where(eye, upper[i, i], 0.0) for i in range(n))
    trace = jnp.sum(jnp.sum(diag_sum, axis=0, keepdims=True), axis=1, keepdims=True)
    ridge = jnp.where(eye, jnp.broadcast_to(RIDGE * (trace / width), (B, B)), 0.0)
    for i in range(n):
        upper[i, i] = upper[i, i] + ridge
    for i in range(n):
        for j in range(n):
            b_ref[i * B : (i + 1) * B, j * B : (j + 1) * B] = moment(PICKS, i, j)

    extra = {}
    for k in range(n):
        inv = leaf_inverse(upper[k, k])
        w_rows = {j: dot_nn(inv, extra[k, j]) for j in range(k)}
        w_rows[k] = inv
        for j in range(n):
            piece = w_rows[j] if j <= k else jnp.zeros((B, B), F32)
            w_ref[k * B : (k + 1) * B, j * B : (j + 1) * B] = piece
        right = {i: dot_nn(inv, upper[k, i]) for i in range(k + 1, n)}
        for i in range(k + 1, n):
            left = right[i].T
            for j in range(i, n):
                upper[i, j] = upper[i, j] - dot_nn(left, right[j])
            for j in range(k + 1):
                update = dot_nn(left, w_rows[j])
                extra[i, j] = extra[i, j] - update if j < k else -update

    comp_block = NC // feat_count
    feat_rows = pl.ds(pl.multiple_of(feat * B, B), B)
    comp_rows = pl.ds(pl.multiple_of(feat * comp_block, comp_block), comp_block)
    lead = jnp.concatenate([w_ref[feat_rows, :], w_ref[comp_rows, :]], axis=0)
    lagged = dot_nn(lead, b_ref[...])
    koop = dot_nt(lagged, w_ref[...])
    koop_ref[...] = koop[:B]
    first_map = w_ref[comp_rows, :].astype(BF16)
    second_map = dot_nn(koop[B:], w_ref[...]).astype(BF16)
    mean_all = jnp.concatenate(mean_row, axis=1)
    offset = jnp.sum(
        mean_all * (first_map.astype(F32) - second_map.astype(F32)), axis=1, keepdims=True
    )

    def apply(maps, frames_block):
        return lax.dot_general(
            maps, frames_block, (((1,), (1,)), ((), ())), preferred_element_type=F32
        )

    step = 256
    for low in range(0, frames, step):
        moments = first + low + lax.broadcasted_iota(jnp.int32, (1, step), 1)
        validity = valid_at(seg_ref, moments)
        backward = apply(second_map, x_ref[low : low + step, :])
        if low + step < frames:
            ahead = x_ref[low + LAG : low + LAG + step, :]
        else:
            ahead = jnp.concatenate([x_ref[low + LAG : frames, :], halo_ref[...]], axis=0)
        forward = apply(first_map, ahead)
        err_ref[:, low : low + step] = (forward - backward - offset) * validity


def shards(features, seg_lengths):
    frames, width = features.shape
    tm_count = lax.axis_size("tm")
    feat_count = lax.axis_size("feat")
    halo = lax.ppermute(features[:LAG], "tm", [(i, i - 1) for i in range(1, tm_count)])
    needed = 2 * PICKS * B + 8
    chunk = -(-needed // (8 * tm_count)) * 8
    vmem = pl.BlockSpec(memory_space=pltpu.VMEM)
    smem = pl.BlockSpec(memory_space=pltpu.SMEM)
    params = pltpu.CompilerParams(vmem_limit_bytes=VMEM_LIMIT)
    partial = pl.pallas_call(
        functools.partial(gram_kernel, chunk),
        out_shape=jax.ShapeDtypeStruct((tm_count * chunk, B), F32),
        in_specs=[smem, vmem, vmem],
        out_specs=vmem,
        scratch_shapes=[pltpu.VMEM((frames, 3 * B), BF16)],
        compiler_params=params,
        name="grams",
    )(seg_lengths, features, halo)
    swapped = lax.all_to_all(partial.reshape(tm_count, chunk, B), "tm", 0, 0)
    summed = jnp.sum(swapped, axis=0)
    spread = jnp.broadcast_to(summed[None], (tm_count * feat_count, chunk, B))
    sums = lax.all_to_all(spread, ("tm", "feat"), 0, 0)
    return pl.pallas_call(
        functools.partial(solve_kernel, tm_count),
        out_shape=[
            jax.ShapeDtypeStruct((width // feat_count, width), F32),
            jax.ShapeDtypeStruct((NC // feat_count, frames), F32),
        ],
        in_specs=[smem, vmem, vmem, vmem],
        out_specs=[vmem, vmem],
        scratch_shapes=[
            pltpu.VMEM((feat_count, tm_count * chunk, B), F32),
            pltpu.VMEM((width, width), F32),
            pltpu.VMEM((width, width), F32),
        ],
        compiler_params=params,
        name="solve",
    )(seg_lengths, sums, features, halo)


def solution(mesh):
    in_specs = (P("tm", None), P())
    out_specs = (P("feat", None), P("feat", "tm"))
    return jax.shard_map(shards, mesh=mesh, in_specs=in_specs, out_specs=out_specs, check_vma=False)
```

```python
import jax
import jax.numpy as jnp
from jax import lax
from jax.experimental import pallas as pl
from jax.experimental.pallas import tpu as pltpu
from jax.sharding import PartitionSpec as P

LAG = 64
NC = 128
RIDGE = 0.05
HIGHEST = lax.Precision.HIGHEST
B = 128
PICKED = 2 * B + B // 2
LOADS = 8
AHEAD = 2
F32 = jnp.float32
BF16 = jnp.bfloat16
VMEM_LIMIT = 48 * 2**20


def dot_nn(left, right):
    return jnp.dot(left, right, precision=HIGHEST, preferred_element_type=F32)


def dot_nt(left, right):
    return lax.dot_general(
        left, right, (((1,), (1,)), ((), ())), precision=HIGHEST, preferred_element_type=F32
    )


def contract(left_rows, right_rows):
    return lax.dot_general(
        left_rows, right_rows, (((0,), (0,)), ((), ())), preferred_element_type=F32
    )


def valid_at(seg_ref, moments):
    def step(k, carry):
        end, crossing = carry
        end = end + seg_ref[k]
        hit = (end > moments) & (end <= moments + LAG)
        return end, jnp.where(hit, 1.0, crossing)

    zero = jnp.zeros(moments.shape, F32)
    _, crossing = lax.fori_loop(0, seg_ref.shape[0], step, (jnp.int32(0), zero))
    return 1.0 - crossing


def own_block(back):
    feat_count = lax.axis_size("y") * lax.axis_size("c")
    feat = lax.axis_index("y") * lax.axis_size("c") + lax.axis_index("c")
    block = lax.rem(feat - back + feat_count, feat_count)
    return pl.ds(pl.multiple_of(block * B, B), B)


def half_block(square):
    feat = lax.axis_index("y") * lax.axis_size("c") + lax.axis_index("c")
    return jnp.where(feat < 2, square.T[: B // 2], square[B // 2 :])


def frame_start(frames):
    return (lax.axis_index("z") * lax.axis_size("x") + lax.axis_index("x")) * frames


def gram_kernel(seg_hbm, x_hbm, out_ref, tail_ref, total_ref, seg_ref, x_ref, z_ref, sems):
    frames = x_ref.shape[0]
    groups = frames // B
    per = frames // LOADS
    lengths = pltpu.make_async_copy(seg_hbm, seg_ref, sems.at[LOADS])
    lengths.start()
    copies = []
    for c in range(LOADS):
        part = pl.ds(c * per, per)
        copies.append(pltpu.make_async_copy(x_hbm.at[part], x_ref.at[part], sems.at[c]))
        copies[c].start()
    first = frame_start(frames)
    cols = own_block(0)
    lengths.wait()
    moments = (
        first
        + lax.broadcasted_iota(jnp.int32, (groups, B), 0) * B
        + lax.broadcasted_iota(jnp.int32, (groups, B), 1)
    )
    ahead = valid_at(seg_ref, moments)
    behind = jnp.where(moments >= LAG, valid_at(seg_ref, moments - LAG), 0.0)
    local_behind = jnp.where(moments - first >= LAG, behind, 0.0)
    stacked = jnp.concatenate(
        [ahead, local_behind, ahead + behind, jnp.zeros((B - 3 * groups, B), F32)], axis=0
    )
    columns = stacked.T

    def weight(row):
        return jnp.broadcast_to(columns[:, row : row + 1], (B, B))

    total = jnp.zeros((8, B), F32)
    half = B - LAG
    copies[0].wait()
    for c in range(LOADS):
        if c + 1 < LOADS:
            copies[c + 1].wait()
        for g in range(c * per // B, (c + 1) * per // B):
            low = g * B
            own = x_ref[low : low + B, cols].astype(F32)
            if g + 1 < groups:
                later = x_ref[low + LAG : low + LAG + B, cols].astype(F32)
            else:
                later = jnp.concatenate(
                    [x_ref[low + LAG : low + B, cols].astype(F32), jnp.zeros((LAG, B), F32)], axis=0
                )
            if g > 0:
                earlier = x_ref[low - LAG : low - LAG + B, cols].astype(F32)
            else:
                earlier = jnp.concatenate(
                    [jnp.zeros((LAG, B), F32), x_ref[0:half, cols].astype(F32)], axis=0
                )
            weighted = own * weight(2 * groups + g)
            z_ref[low : low + B, 0:B] = weighted.astype(BF16)
            z_ref[low : low + B, B : 2 * B] = (later * weight(g)).astype(BF16)
            z_ref[low : low + B, 2 * B : 3 * B] = (earlier * weight(groups + g)).astype(BF16)
            for part in range(B // 8):
                total = total + weighted[8 * part : 8 * part + 8]
    last = x_ref[frames - LAG : frames, :].astype(F32)
    tail_weight = jnp.concatenate([weight(groups - 1)[half:]] * (last.shape[1] // B), axis=1)
    tail_ref[...] = (last * tail_weight).astype(BF16)
    total_ref[...] = jnp.broadcast_to(jnp.sum(total, axis=0, keepdims=True), (8, B))
    for back in range(3):
        prod = contract(x_ref[:, own_block(back)], z_ref[...])
        for base, gram in ((0, prod[:, :B]), (PICKED, prod[:, B : 2 * B] + prod[:, 2 * B :])):
            if back < 2:
                out_ref[base + back * B : base + (back + 1) * B, :] = gram
            else:
                out_ref[base + 2 * B : base + PICKED, :] = half_block(gram)
    if out_ref.shape[0] > 2 * PICKED:
        out_ref[2 * PICKED :, :] = jnp.zeros((out_ref.shape[0] - 2 * PICKED, B), F32)


def sum_places():
    row = lax.broadcasted_iota(jnp.int32, (B, B), 0)
    lane = lax.broadcasted_iota(jnp.int32, (B, B), 1)
    return row, lane, ((row == B - 1) & (lane < B - 1)) | ((row == B - 2) & (lane == 0))


def edge_kernel(part_ref, tail_ref, total_ref, halo_ref, out_ref):
    cols = own_block(0)
    extra = [
        contract(tail_ref[:, own_block(back)], halo_ref[:, cols])
        + contract(halo_ref[:, own_block(back)], tail_ref[:, cols])
        for back in range(3)
    ]
    lows = [PICKED, PICKED + B, PICKED + 2 * B]
    out_ref[:PICKED, :] = part_ref[:PICKED, :]
    row, lane, places = sum_places()
    total = jnp.broadcast_to(total_ref[0:1, :], (B, B))
    total = jnp.where(row == B - 1, total, jnp.broadcast_to(total[:, B - 1 :], (B, B)))
    own = part_ref[lows[0] : lows[1], :] + extra[0]
    out_ref[lows[0] : lows[1], :] = jnp.where(places, total, own)
    out_ref[lows[1] : lows[2], :] = part_ref[lows[1] : lows[2], :] + extra[1]
    high = lows[2] + B // 2
    out_ref[lows[2] : high, :] = part_ref[lows[2] : high, :] + half_block(extra[2])
    if out_ref.shape[0] > high:
        out_ref[high:, :] = part_ref[high:, :]


def across(tile, lane):
    return jnp.broadcast_to(tile[:, lane : lane + 1], tile.shape)


def down(tile, row):
    return jnp.broadcast_to(tile[row : row + 1, :], tile.shape)


def leaf_inverse(square):
    count = square.shape[0] // 8
    lanes = lax.broadcasted_iota(jnp.int32, (8, B), 1)
    subs = lax.broadcasted_iota(jnp.int32, (8, B), 0)
    rows = [square[8 * i : 8 * i + 8, :] for i in range(count)]
    result = []
    carried = {}
    for b in range(count):
        block = (lanes >= 8 * b) & (lanes < 8 * b + 8)
        cols = {
            k: carried[k] if k in carried else [across(rows[k], 8 * b + j) for j in range(8)]
            for k in range(b, count)
        }
        direct = range(b + 1, min(count, b + AHEAD + 1))
        coming = {k: [across(rows[k], 8 * b + 8 + j) for j in range(8)] for k in direct}
        rows[b] = jnp.where(block, jnp.where(lanes - 8 * b == subs, 1.0, 0.0), rows[b])
        for k in range(b + 1, count):
            rows[k] = jnp.where(block, 0.0, rows[k])
        panel = cols[b]
        top = rows[b]
        pivots = None
        for i in range(8):
            pivot = down(panel[i], i)
            recip = 1.0 / pivot
            pivots = pivot if pivots is None else jnp.where(subs == i, pivot, pivots)
            factor = jnp.where(subs > i, panel[i] * recip, 0.0)
            line = down(top, i)
            split = [down(panel[i], j) if j > i else None for j in range(8)]
            for j in range(i + 1, 8):
                panel[j] = panel[j] - factor * split[j]
            if i < 7:
                top = top - factor * line
            if direct:
                right = [down(cols[b + 1][i], j) for j in range(8)]
            for k in direct:
                gain = cols[k][i] * recip
                for j in range(8):
                    coming[k][j] = coming[k][j] - gain * right[j]
                for j in range(i + 1, 8):
                    cols[k][j] = cols[k][j] - gain * split[j]
                rows[k] = rows[k] - gain * line
        result.append(jnp.where(lanes < 8 * b + 8, top * lax.rsqrt(pivots), 0.0))
        if b + AHEAD + 1 < count:
            recips = 1.0 / pivots
            solved = top * recips
            for k in range(7, 0, -1):
                back = jnp.where(subs < k, panel[k] * recips, 0.0)
                solved = solved - back * down(solved, k)
            lines = [down(solved, j) for j in range(8)]
            for k in range(b + AHEAD + 1, count):
                p = [cols[k][j] * lines[j] for j in range(8)]
                rows[k] = rows[k] - (((p[0] + p[1]) + (p[2] + p[3])) + ((p[4] + p[5]) + (p[6] + p[7])))
        carried = coming
    return jnp.concatenate(result, axis=0)


def solve_kernel(seg_ref, *refs):
    sums_refs, (x_ref, halo_ref, koop_hbm, err_hbm) = refs[:8], refs[8:12]
    koop_ref, err_ref, flat_ref, w_ref, b_ref, sems = refs[12:]
    frames, width = x_ref.shape
    n = feat_count = width // B
    lines, chunk = sums_refs[0].shape[:2]
    first = frame_start(frames)
    x, y, c = lax.axis_index("x"), lax.axis_index("y"), lax.axis_index("c")
    feat = y * 2 + c
    for at, sums_ref in enumerate(sums_refs):
        flip_c, flip_x, flip_y = at // 4, (at // 2) % 2, at % 2
        source = (y ^ flip_y) * 2 + (c ^ flip_c)
        for line in range(lines):
            low = pl.multiple_of((line * 2 + (x ^ flip_x)) * chunk, 8)
            flat_ref[source, pl.ds(low, chunk), :] = sums_ref[line]

    def add_pairs(k, total):
        return total + jnp.maximum(seg_ref[k] - LAG, 0)

    pairs = lax.fori_loop(0, seg_ref.shape[0], add_pairs, jnp.int32(0))
    ones = jnp.ones((8, B), F32)
    inv_pairs = (1.0 / (ones * (2.0 * pairs.astype(F32))))[0:1, :]
    row, lane, places = sum_places()
    mean_row = []
    for f in range(n):
        packed = flat_ref[f, PICKED : PICKED + B, :]
        sums = jnp.where(
            lane[:1] < B - 1, packed[B - 1 :], jnp.broadcast_to(packed[B - 2 : B - 1, :1], (1, B))
        )
        mean_row.append(sums * inv_pairs)
        flat_ref[f, PICKED : PICKED + B, :] = jnp.where(places, packed.T, packed)
    mean_col = [jnp.broadcast_to(mean_row[f], (B, B)).T for f in range(n)]

    def summed(base, i, j):
        back = (j - i) % n
        if back < 2:
            return flat_ref[j, base + back * B : base + (back + 1) * B, :]
        if i < j and back == 2:
            low = base + 2 * B
            pieces = [flat_ref[f, low : low + B // 2, :] for f in (i, j)]
            return jnp.concatenate(pieces, axis=0)
        return summed(base, j, i).T

    def moment(base, i, j):
        return summed(base, i, j) * inv_pairs - mean_col[i] * mean_row[j]

    eye = row == lane
    upper = {(i, j): moment(0, i, j) for i in range(n) for j in range(i, n)}
    diag_sum = sum(jnp.where(eye, upper[i, i], 0.0) for i in range(n))
    trace = jnp.sum(jnp.sum(diag_sum, axis=0, keepdims=True), axis=1, keepdims=True)
    ridge = jnp.where(eye, jnp.broadcast_to(RIDGE * (trace / width), (B, B)), 0.0)
    for i in range(n):
        upper[i, i] = upper[i, i] + ridge
    for i in range(n):
        for j in range(n):
            b_ref[i * B : (i + 1) * B, j * B : (j + 1) * B] = moment(PICKED, i, j)

    groups = frames // B
    moments = (
        first
        + lax.broadcasted_iota(jnp.int32, (groups, B), 0) * B
        + lax.broadcasted_iota(jnp.int32, (groups, B), 1)
    )
    validity = valid_at(seg_ref, moments)
    comp_block = NC // feat_count
    comp_rows = pl.ds(pl.multiple_of(feat * comp_block, comp_block), comp_block)
    step = 2 * B

    def apply(maps, frames_block):
        return lax.dot_general(
            maps, frames_block, (((1,), (1,)), ((), ())), preferred_element_type=F32
        )

    extra = {}
    for k in range(n):
        inv = leaf_inverse(upper[k, k])
        w_rows = {j: dot_nn(inv, extra[k, j]) for j in range(k)}
        w_rows[k] = inv
        for j in range(n):
            piece = w_rows[j] if j <= k else jnp.zeros((B, B), F32)
            w_ref[k * B : (k + 1) * B, j * B : (j + 1) * B] = piece
        right = {i: dot_nn(inv, upper[k, i]) for i in range(k + 1, n)}
        for i in range(k + 1, n):
            left = right[i].T
            for j in range(i, n):
                upper[i, j] = upper[i, j] - dot_nn(left, right[j])
            for j in range(k + 1):
                update = dot_nn(left, w_rows[j])
                extra[i, j] = extra[i, j] - update if j < k else -update
        if k == 0:
            first_map = w_ref[comp_rows, :].astype(BF16)
            for low in range(0, frames, step):
                if low + step < frames:
                    ahead = x_ref[low + LAG : low + LAG + step, :B]
                else:
                    ahead = jnp.concatenate(
                        [x_ref[low + LAG : frames, :B], halo_ref[:, :B]], axis=0
                    )
                err_ref[:, low : low + step] = apply(first_map[:, :B], ahead)

    feat_rows = pl.ds(pl.multiple_of(feat * B, B), B)
    lead = jnp.concatenate([w_ref[feat_rows, :], w_ref[comp_rows, :]], axis=0)
    lagged = dot_nn(lead, b_ref[...])
    koop = dot_nt(lagged, w_ref[...])
    koop_ref[...] = koop[:B]
    koop_out = pltpu.make_async_copy(koop_ref, koop_hbm, sems.at[0])
    koop_out.start()
    second_map = dot_nn(koop[B:], w_ref[...]).astype(BF16)
    mean_all = jnp.concatenate(mean_row, axis=1)
    offset = jnp.sum(
        mean_all * (first_map.astype(F32) - second_map.astype(F32)), axis=1, keepdims=True
    )

    parts = 2
    copies = []
    for part in range(parts):
        span = slice(part * frames // parts, (part + 1) * frames // parts)
        for low in range(span.start, span.stop, step):
            backward = apply(second_map, x_ref[low : low + step, :])
            residual = err_ref[:, low : low + step] - backward - offset
            for at in range(step // B):
                g = low // B + at
                keep = jnp.broadcast_to(validity[g : g + 1], (comp_block, B))
                err_ref[:, g * B : (g + 1) * B] = residual[:, at * B : (at + 1) * B] * keep
        copies.append(
            pltpu.make_async_copy(err_ref.at[:, span], err_hbm.at[:, span], sems.at[1 + part])
        )
        copies[part].start()
    koop_out.wait()
    for copy in copies:
        copy.wait()


def swap(shard, *axes):
    last = 2 ** len(axes) - 1
    return lax.ppermute(shard, axes, [(i, last - i) for i in range(last + 1)])


def shards(features, seg_lengths):
    frames, width = features.shape
    line_count = lax.axis_size("z")
    tm_count = line_count * lax.axis_size("x")
    feat_count = lax.axis_size("y") * lax.axis_size("c")
    halo = lax.ppermute(features[:LAG], ("z", "x"), [(i, i - 1) for i in range(1, tm_count)])
    chunk = -(-2 * PICKED // (8 * tm_count)) * 8
    vmem = pl.BlockSpec(memory_space=pltpu.VMEM)
    smem = pl.BlockSpec(memory_space=pltpu.SMEM)
    params = pltpu.CompilerParams(vmem_limit_bytes=VMEM_LIMIT)
    anywhere = pl.BlockSpec(memory_space=pl.ANY)
    partial, tail, total = pl.pallas_call(
        gram_kernel,
        out_shape=[
            jax.ShapeDtypeStruct((tm_count * chunk, B), F32),
            jax.ShapeDtypeStruct((LAG, width), BF16),
            jax.ShapeDtypeStruct((8, B), F32),
        ],
        in_specs=[anywhere, anywhere],
        out_specs=[vmem, vmem, vmem],
        scratch_shapes=[
            pltpu.SMEM(seg_lengths.shape, jnp.int32),
            pltpu.VMEM((frames, width), BF16),
            pltpu.VMEM((frames, 3 * B), BF16),
            pltpu.SemaphoreType.DMA((LOADS + 1,)),
        ],
        compiler_params=pltpu.CompilerParams(vmem_limit_bytes=53 * 2**20),
        cost_estimate=pl.CostEstimate(
            flops=2 * frames * 9 * B * B, bytes_accessed=frames * width * 2, transcendentals=0
        ),
        name="grams",
    )(seg_lengths, features)
    partial = pl.pallas_call(
        edge_kernel,
        out_shape=jax.ShapeDtypeStruct((tm_count * chunk, B), F32),
        in_specs=[vmem] * 4,
        out_specs=vmem,
        compiler_params=params,
        name="edges",
    )(partial, tail, total, halo)
    swapped = lax.all_to_all(partial.reshape(tm_count, chunk, B), ("z", "x"), 0, 0)
    summed = jnp.sum(swapped, axis=0)
    spread = jnp.broadcast_to(summed[None], (line_count, chunk, B))
    line = lax.all_to_all(spread, "z", 0, 0)
    held = [line, swap(line, "y"), swap(line, "x"), swap(line, "x", "y")]
    held = held + [swap(part, "c") for part in held]
    return pl.pallas_call(
        solve_kernel,
        out_shape=[
            jax.ShapeDtypeStruct((width // feat_count, width), F32),
            jax.ShapeDtypeStruct((NC // feat_count, frames), F32),
        ],
        in_specs=[smem] + [vmem] * 10,
        out_specs=[anywhere, anywhere],
        scratch_shapes=[
            pltpu.VMEM((width // feat_count, width), F32),
            pltpu.VMEM((NC // feat_count, frames), F32),
            pltpu.VMEM((feat_count, tm_count * chunk, B), F32),
            pltpu.VMEM((width, width), F32),
            pltpu.VMEM((width, width), F32),
            pltpu.SemaphoreType.DMA((3,)),
        ],
        compiler_params=params,
        name="solve",
    )(seg_lengths, *held, features, halo)


def solution(mesh):
    tm, feat = mesh.shape["tm"], mesh.shape["feat"]
    fine = jax.sharding.Mesh(
        mesh.devices.reshape(tm // 2, 2, feat // 2, 2), ("z", "x", "y", "c")
    )
    in_specs = (P(("z", "x"), None), P())
    out_specs = (P(("y", "c"), None), P(("y", "c"), ("z", "x")))
    return jax.shard_map(shards, mesh=fine, in_specs=in_specs, out_specs=out_specs, check_vma=False)
```

```python
import jax
import jax.numpy as jnp
from jax import lax
from jax.experimental import pallas as pl
from jax.experimental.pallas import tpu as pltpu
from jax.sharding import PartitionSpec as P

LAG = 64
NC = 128
RIDGE = 0.05
HIGHEST = lax.Precision.HIGHEST
B = 128
PICKED = 2 * B + B // 2
LOADS = 4
AHEAD = 2
F32 = jnp.float32
BF16 = jnp.bfloat16
VMEM_LIMIT = 48 * 2**20


def dot_nn(left, right):
    return jnp.dot(left, right, precision=HIGHEST, preferred_element_type=F32)


def contract(left_rows, right_rows):
    return lax.dot_general(
        left_rows, right_rows, (((0,), (0,)), ((), ())), preferred_element_type=F32
    )


def valid_at(seg_ref, moments):
    def step(k, carry):
        end, crossing = carry
        end = end + seg_ref[k]
        hit = (end > moments) & (end <= moments + LAG)
        return end, jnp.where(hit, 1.0, crossing)

    zero = jnp.zeros(moments.shape, F32)
    _, crossing = lax.fori_loop(0, seg_ref.shape[0], step, (jnp.int32(0), zero), unroll=True)
    return 1.0 - crossing


def own_block(back):
    feat_count = lax.axis_size("y") * lax.axis_size("c")
    feat = lax.axis_index("y") * lax.axis_size("c") + lax.axis_index("c")
    block = lax.rem(feat - back + feat_count, feat_count)
    return pl.ds(pl.multiple_of(block * B, B), B)


def half_block(square):
    feat = lax.axis_index("y") * lax.axis_size("c") + lax.axis_index("c")
    return jnp.where(feat < 2, square.T[: B // 2], square[B // 2 :])


def frame_start(frames):
    return (lax.axis_index("z") * lax.axis_size("x") + lax.axis_index("x")) * frames


def gram_kernel(seg_hbm, x_hbm, out_ref, tail_ref, total_ref, seg_ref, x_ref, z_ref, sems):
    frames = x_ref.shape[0]
    groups = frames // B
    per = frames // LOADS
    lengths = pltpu.make_async_copy(seg_hbm, seg_ref, sems.at[LOADS])
    lengths.start()
    copies = []
    for c in range(LOADS):
        part = pl.ds(c * per, per)
        copies.append(pltpu.make_async_copy(x_hbm.at[part], x_ref.at[part], sems.at[c]))
        copies[c].start()
    first = frame_start(frames)
    cols = own_block(0)
    lengths.wait()
    moments = (
        first
        + lax.broadcasted_iota(jnp.int32, (groups, B), 0) * B
        + lax.broadcasted_iota(jnp.int32, (groups, B), 1)
    )
    ahead = valid_at(seg_ref, moments)
    behind = jnp.where(moments >= LAG, valid_at(seg_ref, moments - LAG), 0.0)
    local_behind = jnp.where(moments - first >= LAG, behind, 0.0)
    stacked = jnp.concatenate(
        [ahead, local_behind, ahead + behind, jnp.zeros((B - 3 * groups, B), F32)], axis=0
    )
    columns = stacked.T

    def weight(row):
        return jnp.broadcast_to(columns[:, row : row + 1], (B, B))

    total = jnp.zeros((8, B), F32)
    half = B - LAG
    copies[0].wait()
    for c in range(LOADS):
        if c + 1 < LOADS:
            copies[c + 1].wait()
        for g in range(c * per // B, (c + 1) * per // B):
            low = g * B
            own = x_ref[low : low + B, cols].astype(F32)
            if g + 1 < groups:
                later = x_ref[low + LAG : low + LAG + B, cols].astype(F32)
            else:
                later = jnp.concatenate(
                    [x_ref[low + LAG : low + B, cols].astype(F32), jnp.zeros((LAG, B), F32)], axis=0
                )
            if g > 0:
                earlier = x_ref[low - LAG : low - LAG + B, cols].astype(F32)
            else:
                earlier = jnp.concatenate(
                    [jnp.zeros((LAG, B), F32), x_ref[0:half, cols].astype(F32)], axis=0
                )
            weighted = own * weight(2 * groups + g)
            z_ref[low : low + B, 0:B] = weighted.astype(BF16)
            z_ref[low : low + B, B : 2 * B] = (later * weight(g)).astype(BF16)
            z_ref[low : low + B, 2 * B : 3 * B] = (earlier * weight(groups + g)).astype(BF16)
            for part in range(B // 8):
                total = total + weighted[8 * part : 8 * part + 8]
    last = x_ref[frames - LAG : frames, :].astype(F32)
    tail_weight = jnp.concatenate([weight(groups - 1)[half:]] * (last.shape[1] // B), axis=1)
    tail_ref[...] = (last * tail_weight).astype(BF16)
    total_ref[...] = jnp.broadcast_to(jnp.sum(total, axis=0, keepdims=True), (8, B))
    for back in range(3):
        prod = contract(x_ref[:, own_block(back)], z_ref[...])
        for base, gram in ((0, prod[:, :B]), (PICKED, prod[:, B : 2 * B] + prod[:, 2 * B :])):
            if back < 2:
                out_ref[base + back * B : base + (back + 1) * B, :] = gram
            else:
                out_ref[base + 2 * B : base + PICKED, :] = half_block(gram)
    if out_ref.shape[0] > 2 * PICKED:
        out_ref[2 * PICKED :, :] = jnp.zeros((out_ref.shape[0] - 2 * PICKED, B), F32)


def sum_places():
    row = lax.broadcasted_iota(jnp.int32, (B, B), 0)
    lane = lax.broadcasted_iota(jnp.int32, (B, B), 1)
    return row, lane, ((row == B - 1) & (lane < B - 1)) | ((row == B - 2) & (lane == 0))


def edge_kernel(part_ref, tail_ref, total_ref, halo_ref, out_ref):
    cols = own_block(0)
    extra = [
        contract(tail_ref[:, own_block(back)], halo_ref[:, cols])
        + contract(halo_ref[:, own_block(back)], tail_ref[:, cols])
        for back in range(3)
    ]
    lows = [PICKED, PICKED + B, PICKED + 2 * B]
    out_ref[:PICKED, :] = part_ref[:PICKED, :]
    row, lane, places = sum_places()
    total = jnp.broadcast_to(total_ref[0:1, :], (B, B))
    total = jnp.where(row == B - 1, total, jnp.broadcast_to(total[:, B - 1 :], (B, B)))
    own = part_ref[lows[0] : lows[1], :] + extra[0]
    out_ref[lows[0] : lows[1], :] = jnp.where(places, total, own)
    out_ref[lows[1] : lows[2], :] = part_ref[lows[1] : lows[2], :] + extra[1]
    high = lows[2] + B // 2
    out_ref[lows[2] : high, :] = part_ref[lows[2] : high, :] + half_block(extra[2])
    if out_ref.shape[0] > high:
        out_ref[high:, :] = part_ref[high:, :]


def across(tile, lane):
    return jnp.broadcast_to(tile[:, lane : lane + 1], tile.shape)


def down(tile, row):
    return jnp.broadcast_to(tile[row : row + 1, :], tile.shape)


def leaf_inverse(square):
    count = square.shape[0] // 8
    lanes = lax.broadcasted_iota(jnp.int32, (8, B), 1)
    subs = lax.broadcasted_iota(jnp.int32, (8, B), 0)
    rows = [square[8 * i : 8 * i + 8, :] for i in range(count)]
    result = []
    carried = {}
    for b in range(count):
        block = (lanes >= 8 * b) & (lanes < 8 * b + 8)
        cols = {
            k: carried[k] if k in carried else [across(rows[k], 8 * b + j) for j in range(8)]
            for k in range(b, count)
        }
        direct = range(b + 1, min(count, b + AHEAD + 1))
        coming = {k: [across(rows[k], 8 * b + 8 + j) for j in range(8)] for k in direct}
        rows[b] = jnp.where(block, jnp.where(lanes - 8 * b == subs, 1.0, 0.0), rows[b])
        for k in range(b + 1, count):
            rows[k] = jnp.where(block, 0.0, rows[k])
        panel = cols[b]
        top = rows[b]
        pivots = None
        for i in range(8):
            pivot = down(panel[i], i)
            recip = 1.0 / pivot
            pivots = pivot if pivots is None else jnp.where(subs == i, pivot, pivots)
            factor = jnp.where(subs > i, panel[i] * recip, 0.0)
            line = down(top, i)
            split = [down(panel[i], j) if j > i else None for j in range(8)]
            for j in range(i + 1, 8):
                panel[j] = panel[j] - factor * split[j]
            if i < 7:
                top = top - factor * line
            if direct:
                right = [down(cols[b + 1][i], j) for j in range(8)]
            for k in direct:
                gain = cols[k][i] * recip
                for j in range(8):
                    coming[k][j] = coming[k][j] - gain * right[j]
                for j in range(i + 1, 8):
                    cols[k][j] = cols[k][j] - gain * split[j]
                rows[k] = rows[k] - gain * line
        result.append(jnp.where(lanes < 8 * b + 8, top * lax.rsqrt(pivots), 0.0))
        if b + AHEAD + 1 < count:
            recips = 1.0 / pivots
            solved = top * recips
            for k in range(7, 0, -1):
                back = jnp.where(subs < k, panel[k] * recips, 0.0)
                solved = solved - back * down(solved, k)
            lines = [down(solved, j) for j in range(8)]
            for k in range(b + AHEAD + 1, count):
                p = [cols[k][j] * lines[j] for j in range(8)]
                rows[k] = rows[k] - (((p[0] + p[1]) + (p[2] + p[3])) + ((p[4] + p[5]) + (p[6] + p[7])))
        carried = coming
    return jnp.concatenate(result, axis=0)


def solve_kernel(seg_ref, *refs):
    sums_refs, (x_ref, halo_ref, koop_hbm, err_hbm) = refs[:8], refs[8:12]
    koop_ref, err_ref, flat_ref, w_ref, wt_ref, t_ref, sems = refs[12:]
    frames, width = x_ref.shape
    n = feat_count = width // B
    lines, chunk = sums_refs[0].shape[:2]
    first = frame_start(frames)
    z, x, y, c = [lax.axis_index(name) for name in ("z", "x", "y", "c")]
    feat = y * 2 + c
    for at, sums_ref in enumerate(sums_refs):
        flip_c, flip_x, flip_y = at // 4, (at // 2) % 2, at % 2
        source = (y ^ flip_y) * 2 + (c ^ flip_c)
        for line in range(lines):
            low = pl.multiple_of(((z ^ line) * 2 + (x ^ flip_x)) * chunk, 8)
            flat_ref[source, pl.ds(low, chunk), :] = sums_ref[line]

    def add_pairs(k, total):
        return total + jnp.maximum(seg_ref[k] - LAG, 0)

    pairs = lax.fori_loop(0, seg_ref.shape[0], add_pairs, jnp.int32(0), unroll=True)
    ones = jnp.ones((8, B), F32)
    inv_pairs = (1.0 / (ones * (2.0 * pairs.astype(F32))))[0:1, :]
    row, lane, places = sum_places()
    mean_row = []
    for f in range(n):
        packed = flat_ref[f, PICKED : PICKED + B, :]
        sums = jnp.where(
            lane[:1] < B - 1, packed[B - 1 :], jnp.broadcast_to(packed[B - 2 : B - 1, :1], (1, B))
        )
        mean_row.append(sums * inv_pairs)
        flat_ref[f, PICKED : PICKED + B, :] = jnp.where(places, packed.T, packed)
    mean_col = [jnp.broadcast_to(mean_row[f], (B, B)).T for f in range(n)]

    def summed(base, i, j):
        back = (j - i) % n
        if back < 2:
            return flat_ref[j, base + back * B : base + (back + 1) * B, :]
        if i < j and back == 2:
            low = base + 2 * B
            pieces = [flat_ref[f, low : low + B // 2, :] for f in (i, j)]
            return jnp.concatenate(pieces, axis=0)
        return summed(base, j, i).T

    def moment(base, i, j):
        return summed(base, i, j) * inv_pairs - mean_col[i] * mean_row[j]

    eye = row == lane
    upper = {(i, j): moment(0, i, j) for i in range(n) for j in range(i, n)}
    diag_sum = sum(jnp.where(eye, upper[i, i], 0.0) for i in range(n))
    trace = jnp.sum(jnp.sum(diag_sum, axis=0, keepdims=True), axis=1, keepdims=True)
    ridge = jnp.where(eye, jnp.broadcast_to(RIDGE * (trace / width), (B, B)), 0.0)
    for i in range(n):
        upper[i, i] = upper[i, i] + ridge
    comp_block = NC // feat_count
    comp_rows = pl.ds(pl.multiple_of(feat * comp_block, comp_block), comp_block)
    step = 2 * B

    def apply(maps, frames_block):
        return lax.dot_general(
            maps, frames_block, (((1,), (1,)), ((), ())), preferred_element_type=F32
        )

    extra = {}
    lagged = {}
    for k in range(n):
        inv = leaf_inverse(upper[k, k])
        if k == 0:
            for i in range(n):
                lagged[i] = jnp.concatenate([moment(PICKED, i, j) for j in range(n)], axis=1)
        rest = range(k + 1, n)
        if rest:
            near = dot_nn(inv, upper[k, k + 1])
            left = [near.T]
            upper[k + 1, k + 1] = upper[k + 1, k + 1] - dot_nn(left[0], near)
        others = [upper[k, i] for i in range(k + 2, n)] + ([extra[k]] if k else []) + [lagged[k]]
        others = dot_nn(inv, jnp.concatenate(others, axis=1))
        at = max(n - k - 2, 0) * B
        far = [others[:, i : i + B] for i in range(0, at, B)]
        w_rows = jnp.concatenate([others[:, at : at + k * B], inv], axis=1) if k else inv
        t_rows = others[:, at + k * B :]
        w_ref[k * B : (k + 1) * B, : (k + 1) * B] = w_rows
        wt_ref[: (k + 1) * B, k * B : (k + 1) * B] = w_rows.T
        if k + 1 < n:
            w_ref[k * B : (k + 1) * B, (k + 1) * B :] = jnp.zeros((B, (n - 1 - k) * B), F32)
            wt_ref[(k + 1) * B :, k * B : (k + 1) * B] = jnp.zeros(((n - 1 - k) * B, B), F32)
        t_ref[k * B : (k + 1) * B, :] = t_rows
        if rest:
            left = jnp.concatenate(left + [block.T for block in far], axis=0)
            update = dot_nn(left, jnp.concatenate(far + [w_rows, t_rows], axis=1))
            for i in rest:
                line = update[(i - k - 1) * B : (i - k) * B]
                for j in range(max(i, k + 2), n):
                    upper[i, j] = upper[i, j] - line[:, (j - k - 2) * B : (j - k - 1) * B]
                new = -line[:, at + k * B : at + (k + 1) * B]
                if k:
                    new = jnp.concatenate([extra[i] - line[:, at : at + k * B], new], axis=1)
                extra[i] = new
                lagged[i] = lagged[i] - line[:, at + (k + 1) * B :]
        if k == 0:
            groups = frames // B
            moments = (
                first
                + lax.broadcasted_iota(jnp.int32, (groups, B), 0) * B
                + lax.broadcasted_iota(jnp.int32, (groups, B), 1)
            )
            validity = valid_at(seg_ref, moments)
            first_map = w_ref[comp_rows, :].astype(BF16)
            for low in range(0, frames, step):
                if low + step < frames:
                    ahead = x_ref[low + LAG : low + LAG + step, :B]
                else:
                    ahead = jnp.concatenate(
                        [x_ref[low + LAG : frames, :B], halo_ref[:, :B]], axis=0
                    )
                err_ref[:, low : low + step] = apply(first_map[:, :B], ahead)

    feat_rows = pl.ds(pl.multiple_of(feat * B, B), B)
    lead = jnp.concatenate([t_ref[feat_rows, :], t_ref[comp_rows, :]], axis=0)
    half = width // 2
    low_cols = dot_nn(lead[:, :half], wt_ref[:half, :half])
    koop = jnp.concatenate([low_cols, dot_nn(lead, wt_ref[:, half:])], axis=1)
    koop_ref[...] = koop[:B]
    koop_out = pltpu.make_async_copy(koop_ref, koop_hbm, sems.at[0])
    koop_out.start()
    low_cols = dot_nn(koop[B:], w_ref[:, :half])
    high_cols = dot_nn(koop[B:, half:], w_ref[half:, half:])
    second_map = jnp.concatenate([low_cols, high_cols], axis=1).astype(BF16)
    mean_all = jnp.concatenate(mean_row, axis=1)
    offset = jnp.sum(
        mean_all * (first_map.astype(F32) - second_map.astype(F32)), axis=1, keepdims=True
    )

    parts = 4
    copies = []
    for part in range(parts):
        span = slice(part * frames // parts, (part + 1) * frames // parts)
        for low in range(span.start, span.stop, step):
            backward = apply(second_map, x_ref[low : low + step, :])
            residual = err_ref[:, low : low + step] - backward - offset
            for at in range(step // B):
                g = low // B + at
                keep = jnp.broadcast_to(validity[g : g + 1], (comp_block, B))
                err_ref[:, g * B : (g + 1) * B] = residual[:, at * B : (at + 1) * B] * keep
        copies.append(
            pltpu.make_async_copy(err_ref.at[:, span], err_hbm.at[:, span], sems.at[1 + part])
        )
        copies[part].start()
    koop_out.wait()
    for copy in copies:
        copy.wait()


def swap(shard, *axes):
    last = 2 ** len(axes) - 1
    return lax.ppermute(shard, axes, [(i, last - i) for i in range(last + 1)])


def gather_line(piece):
    count = lax.axis_size("z")
    if count <= 4:
        moved = [
            lax.ppermute(piece, "z", [(i, i ^ m) for i in range(count)]) for m in range(1, count)
        ]
        return jnp.stack([piece] + moved)
    spread = jnp.broadcast_to(piece[None], (count,) + piece.shape)
    order = lax.axis_index("z") ^ jnp.arange(count, dtype=jnp.int32)
    return jnp.take(lax.all_to_all(spread, "z", 0, 0), order, axis=0)


def shards(features, seg_lengths):
    frames, width = features.shape
    line_count = lax.axis_size("z")
    tm_count = line_count * lax.axis_size("x")
    feat_count = lax.axis_size("y") * lax.axis_size("c")
    halo = lax.ppermute(features[:LAG], ("z", "x"), [(i, i - 1) for i in range(1, tm_count)])
    chunk = -(-2 * PICKED // (8 * tm_count)) * 8
    vmem = pl.BlockSpec(memory_space=pltpu.VMEM)
    smem = pl.BlockSpec(memory_space=pltpu.SMEM)
    params = pltpu.CompilerParams(vmem_limit_bytes=VMEM_LIMIT)
    anywhere = pl.BlockSpec(memory_space=pl.ANY)
    partial, tail, total = pl.pallas_call(
        gram_kernel,
        out_shape=[
            jax.ShapeDtypeStruct((tm_count * chunk, B), F32),
            jax.ShapeDtypeStruct((LAG, width), BF16),
            jax.ShapeDtypeStruct((8, B), F32),
        ],
        in_specs=[anywhere, anywhere],
        out_specs=[vmem, vmem, vmem],
        scratch_shapes=[
            pltpu.SMEM(seg_lengths.shape, jnp.int32),
            pltpu.VMEM((frames, width), BF16),
            pltpu.VMEM((frames, 3 * B), BF16),
            pltpu.SemaphoreType.DMA((LOADS + 1,)),
        ],
        compiler_params=pltpu.CompilerParams(vmem_limit_bytes=53 * 2**20),
        cost_estimate=pl.CostEstimate(
            flops=2 * frames * 9 * B * B, bytes_accessed=frames * width * 2, transcendentals=0
        ),
        name="grams",
    )(seg_lengths, features)
    partial = pl.pallas_call(
        edge_kernel,
        out_shape=jax.ShapeDtypeStruct((tm_count * chunk, B), F32),
        in_specs=[vmem] * 4,
        out_specs=vmem,
        compiler_params=params,
        name="edges",
    )(partial, tail, total, halo)
    swapped = lax.all_to_all(partial.reshape(tm_count, chunk, B), ("z", "x"), 0, 0)
    summed = jnp.sum(swapped, axis=0)
    line = gather_line(summed)
    held = [line, swap(line, "y"), swap(line, "x"), swap(line, "x", "y")]
    held = held + [swap(part, "c") for part in held]
    return pl.pallas_call(
        solve_kernel,
        out_shape=[
            jax.ShapeDtypeStruct((width // feat_count, width), F32),
            jax.ShapeDtypeStruct((NC // feat_count, frames), F32),
        ],
        in_specs=[smem] + [vmem] * 10,
        out_specs=[anywhere, anywhere],
        scratch_shapes=[
            pltpu.VMEM((width // feat_count, width), F32),
            pltpu.VMEM((NC // feat_count, frames), F32),
            pltpu.VMEM((feat_count, tm_count * chunk, B), F32),
            pltpu.VMEM((width, width), F32),
            pltpu.VMEM((width, width), F32),
            pltpu.VMEM((width, width), F32),
            pltpu.SemaphoreType.DMA((5,)),
        ],
        compiler_params=params,
        name="solve",
    )(seg_lengths, *held, features, halo)


def solution(mesh):
    tm, feat = mesh.shape["tm"], mesh.shape["feat"]
    fine = jax.sharding.Mesh(
        mesh.devices.reshape(tm // 2, 2, feat // 2, 2), ("z", "x", "y", "c")
    )
    in_specs = (P(("z", "x"), None), P())
    out_specs = (P(("y", "c"), None), P(("y", "c"), ("z", "x")))
    return jax.shard_map(shards, mesh=fine, in_specs=in_specs, out_specs=out_specs, check_vma=False)
```

```python
import jax
import jax.numpy as jnp
from jax import lax
from jax.experimental import pallas as pl
from jax.experimental.pallas import tpu as pltpu
from jax.sharding import PartitionSpec as P

LAG = 64
NC = 128
RIDGE = 0.05
HIGHEST = lax.Precision.HIGHEST
B = 128
PICKED = 2 * B + B // 2
SIDE = PICKED - B
PACKED = 2 * SIDE + B + 8
LOADS = 4
AHEAD = 2
F32 = jnp.float32
BF16 = jnp.bfloat16
VMEM_LIMIT = 48 * 2**20


def dot_nn(left, right):
    return jnp.dot(left, right, precision=HIGHEST, preferred_element_type=F32)


def contract(left_rows, right_rows):
    return lax.dot_general(
        left_rows, right_rows, (((0,), (0,)), ((), ())), preferred_element_type=F32
    )


def valid_at(seg_ref, moments):
    def step(k, carry):
        end, crossing = carry
        end = end + seg_ref[k]
        hit = (end > moments) & (end <= moments + LAG)
        return end, jnp.where(hit, 1.0, crossing)

    zero = jnp.zeros(moments.shape, F32)
    _, crossing = lax.fori_loop(0, seg_ref.shape[0], step, (jnp.int32(0), zero), unroll=True)
    return 1.0 - crossing


def own_block(back):
    feat_count = lax.axis_size("y") * lax.axis_size("c")
    feat = lax.axis_index("y") * lax.axis_size("c") + lax.axis_index("c")
    block = lax.rem(feat - back + feat_count, feat_count)
    return pl.ds(pl.multiple_of(block * B, B), B)


def half_block(square):
    feat = lax.axis_index("y") * lax.axis_size("c") + lax.axis_index("c")
    return jnp.where(feat < 2, square.T[: B // 2], square[B // 2 :])


def frame_start(frames):
    return (lax.axis_index("z") * lax.axis_size("x") + lax.axis_index("x")) * frames


def gram_kernel(seg_hbm, x_hbm, out_ref, tail_ref, total_ref, seg_ref, x_ref, z_ref, sems):
    frames = x_ref.shape[0]
    groups = frames // B
    per = frames // LOADS
    lengths = pltpu.make_async_copy(seg_hbm, seg_ref, sems.at[LOADS])
    lengths.start()
    copies = []
    for c in range(LOADS):
        part = pl.ds(c * per, per)
        copies.append(pltpu.make_async_copy(x_hbm.at[part], x_ref.at[part], sems.at[c]))
        copies[c].start()
    first = frame_start(frames)
    cols = own_block(0)
    lengths.wait()
    moments = (
        first
        + lax.broadcasted_iota(jnp.int32, (groups, B), 0) * B
        + lax.broadcasted_iota(jnp.int32, (groups, B), 1)
    )
    ahead = valid_at(seg_ref, moments)
    start = jnp.where(moments[:8] >= LAG, valid_at(seg_ref, moments[:8] - LAG), 0.0)
    columns = jnp.concatenate([ahead, start, jnp.zeros((B - groups - 8, B), F32)], axis=0).T

    def weight(row):
        return jnp.broadcast_to(columns[:, row : row + 1], (B, B))

    weights = [weight(g) for g in range(groups)]
    first_behind = weight(groups)[:LAG]
    total = jnp.zeros((8, B), F32)
    half = B - LAG
    copies[0].wait()
    for c in range(LOADS):
        if c + 1 < LOADS:
            copies[c + 1].wait()
        for g in range(c * per // B, (c + 1) * per // B):
            low = g * B
            own = x_ref[low : low + B, cols].astype(F32)
            if g + 1 < groups:
                later = x_ref[low + LAG : low + LAG + B, cols].astype(F32)
            else:
                later = jnp.concatenate(
                    [x_ref[low + LAG : low + B, cols].astype(F32), jnp.zeros((LAG, B), F32)], axis=0
                )
            if g > 0:
                earlier = x_ref[low - LAG : low - LAG + B, cols].astype(F32)
            else:
                earlier = jnp.concatenate(
                    [jnp.zeros((LAG, B), F32), x_ref[0:half, cols].astype(F32)], axis=0
                )
            before = weights[g - 1][half:] if g > 0 else jnp.zeros((LAG, B), F32)
            behind = jnp.concatenate([before, weights[g][:half]], axis=0)
            both = jnp.concatenate([before if g > 0 else first_behind, weights[g][:half]], axis=0)
            weighted = own * (weights[g] + both)
            z_ref[low : low + B, 0:B] = weighted.astype(BF16)
            z_ref[low : low + B, B : 2 * B] = (later * weights[g]).astype(BF16)
            z_ref[low : low + B, 2 * B : 3 * B] = (earlier * behind).astype(BF16)
            for part in range(B // 8):
                total = total + weighted[8 * part : 8 * part + 8]
    last = x_ref[frames - LAG : frames, :].astype(F32)
    tail_weight = jnp.concatenate([weights[groups - 1][half:]] * (last.shape[1] // B), axis=1)
    tail_ref[...] = (last * tail_weight).astype(BF16)
    total_ref[...] = jnp.broadcast_to(jnp.sum(total, axis=0, keepdims=True), (8, B))
    for back in range(3):
        prod = contract(x_ref[:, own_block(back)], z_ref[...])
        for base, gram in ((0, prod[:, :B]), (PICKED, prod[:, B : 2 * B] + prod[:, 2 * B :])):
            if back < 2:
                out_ref[base + back * B : base + (back + 1) * B, :] = gram
            else:
                out_ref[base + 2 * B : base + PICKED, :] = half_block(gram)


def square_places():
    return lax.broadcasted_iota(jnp.int32, (B, B), 0), lax.broadcasted_iota(jnp.int32, (B, B), 1)


def edge_kernel(part_ref, tail_ref, total_ref, halo_ref, out_ref):
    cols = own_block(0)
    extra = [
        contract(tail_ref[:, own_block(back)], halo_ref[:, cols])
        + contract(halo_ref[:, own_block(back)], tail_ref[:, cols])
        for back in range(3)
    ]
    out_ref[:SIDE, :] = part_ref[B:PICKED, :]
    out_ref[SIDE : SIDE + B, :] = part_ref[PICKED + B : PICKED + 2 * B, :] + extra[1]
    out_ref[SIDE + B : 2 * SIDE, :] = part_ref[PICKED + 2 * B :, :] + half_block(extra[2])
    row, lane = square_places()
    own = part_ref[PICKED : PICKED + B, :] + extra[0]
    out_ref[2 * SIDE : 2 * SIDE + B, :] = jnp.where(lane >= row, part_ref[:B, :], own)
    diag = jnp.sum(jnp.where(lane == row, own, 0.0), axis=0, keepdims=True)
    last = lax.broadcasted_iota(jnp.int32, (8, B), 0)
    last = jnp.where(last == 0, diag, jnp.where(last == 1, total_ref[...], 0.0))
    out_ref[2 * SIDE + B : PACKED, :] = last
    if out_ref.shape[0] > PACKED:
        out_ref[PACKED:, :] = jnp.zeros((out_ref.shape[0] - PACKED, B), F32)


def across(tile, lane):
    return jnp.broadcast_to(tile[:, lane : lane + 1], tile.shape)


def down(tile, row):
    return jnp.broadcast_to(tile[row : row + 1, :], tile.shape)


def leaf_inverse(square):
    count = square.shape[0] // 8
    lanes = lax.broadcasted_iota(jnp.int32, (8, B), 1)
    subs = lax.broadcasted_iota(jnp.int32, (8, B), 0)
    rows = [square[8 * i : 8 * i + 8, :] for i in range(count)]
    result = []
    carried = {}
    for b in range(count):
        block = (lanes >= 8 * b) & (lanes < 8 * b + 8)
        cols = {
            k: carried[k] if k in carried else [across(rows[k], 8 * b + j) for j in range(8)]
            for k in range(b, count)
        }
        direct = range(b + 1, min(count, b + AHEAD + 1))
        coming = {k: [across(rows[k], 8 * b + 8 + j) for j in range(8)] for k in direct}
        rows[b] = jnp.where(block, jnp.where(lanes - 8 * b == subs, 1.0, 0.0), rows[b])
        for k in range(b + 1, count):
            rows[k] = jnp.where(block, 0.0, rows[k])
        panel = cols[b]
        top = rows[b]
        pivots = None
        for i in range(8):
            pivot = down(panel[i], i)
            recip = 1.0 / pivot
            pivots = pivot if pivots is None else jnp.where(subs == i, pivot, pivots)
            factor = jnp.where(subs > i, panel[i] * recip, 0.0)
            line = down(top, i)
            split = [down(panel[i], j) if j > i else None for j in range(8)]
            for j in range(i + 1, 8):
                panel[j] = panel[j] - factor * split[j]
            if i < 7:
                top = top - factor * line
            if direct:
                right = [down(cols[b + 1][i], j) for j in range(8)]
            for k in direct:
                gain = cols[k][i] * recip
                for j in range(8):
                    coming[k][j] = coming[k][j] - gain * right[j]
                for j in range(i + 1, 8):
                    cols[k][j] = cols[k][j] - gain * split[j]
                rows[k] = rows[k] - gain * line
        result.append(jnp.where(lanes < 8 * b + 8, top * lax.rsqrt(pivots), 0.0))
        if b + AHEAD + 1 < count:
            recips = 1.0 / pivots
            solved = top * recips
            for k in range(7, 0, -1):
                back = jnp.where(subs < k, panel[k] * recips, 0.0)
                solved = solved - back * down(solved, k)
            lines = [down(solved, j) for j in range(8)]
            for k in range(b + AHEAD + 1, count):
                p = [cols[k][j] * lines[j] for j in range(8)]
                rows[k] = rows[k] - (((p[0] + p[1]) + (p[2] + p[3])) + ((p[4] + p[5]) + (p[6] + p[7])))
        carried = coming
    return jnp.concatenate(result, axis=0)


def solve_kernel(seg_ref, *refs):
    sums_refs, (x_ref, halo_ref, koop_hbm, err_hbm) = refs[:8], refs[8:12]
    koop_ref, err_ref, flat_ref, w_ref, wt_ref, t_ref, sems = refs[12:]
    frames, width = x_ref.shape
    n = feat_count = width // B
    lines, chunk = sums_refs[0].shape[:2]
    first = frame_start(frames)
    z, x, y, c = [lax.axis_index(name) for name in ("z", "x", "y", "c")]
    feat = y * 2 + c
    for at, sums_ref in enumerate(sums_refs):
        flip_c, flip_x, flip_y = at // 4, (at // 2) % 2, at % 2
        source = (y ^ flip_y) * 2 + (c ^ flip_c)
        for line in range(lines):
            low = pl.multiple_of(((z ^ line) * 2 + (x ^ flip_x)) * chunk, 8)
            flat_ref[source, pl.ds(low, chunk), :] = sums_ref[line]

    def add_pairs(k, total):
        return total + jnp.maximum(seg_ref[k] - LAG, 0)

    pairs = lax.fori_loop(0, seg_ref.shape[0], add_pairs, jnp.int32(0), unroll=True)
    ones = jnp.ones((8, B), F32)
    inv_pairs = (1.0 / (ones * (2.0 * pairs.astype(F32))))[0:1, :]
    row, lane = square_places()
    low = 2 * SIDE + B
    mean_row = [flat_ref[f, low + 1 : low + 2, :] * inv_pairs for f in range(n)]
    mean_col = [jnp.broadcast_to(mean_row[f], (B, B)).T for f in range(n)]

    squares = [flat_ref[f, 2 * SIDE : 2 * SIDE + B, :] for f in range(n)]
    turned = [square.T for square in squares]

    def summed(base, i, j):
        back = (j - i) % n
        if back == 0 and base == 0:
            return jnp.where(lane >= row, squares[i], turned[i])
        if back == 0:
            diag = jnp.broadcast_to(flat_ref[i, 2 * SIDE + B : 2 * SIDE + B + 1, :], (B, B))
            return jnp.where(lane == row, diag, jnp.where(lane < row, squares[i], turned[i]))
        if back == 1:
            return flat_ref[j, base : base + B, :]
        if i < j and back == 2:
            pieces = [flat_ref[f, base + B : base + SIDE, :] for f in (i, j)]
            return jnp.concatenate(pieces, axis=0)
        return summed(base, j, i).T

    def moment(base, i, j):
        return summed(base, i, j) * inv_pairs - mean_col[i] * mean_row[j]

    eye = row == lane
    upper = {(i, j): moment(0, i, j) for i in range(n) for j in range(i, n)}
    diag_sum = sum(jnp.where(eye, upper[i, i], 0.0) for i in range(n))
    trace = jnp.sum(jnp.sum(diag_sum, axis=0, keepdims=True), axis=1, keepdims=True)
    ridge = jnp.where(eye, jnp.broadcast_to(RIDGE * (trace / width), (B, B)), 0.0)
    for i in range(n):
        upper[i, i] = upper[i, i] + ridge
    comp_block = NC // feat_count
    comp_rows = pl.ds(pl.multiple_of(feat * comp_block, comp_block), comp_block)
    step = 2 * B

    def apply(maps, frames_block):
        return lax.dot_general(
            maps, frames_block, (((1,), (1,)), ((), ())), preferred_element_type=F32
        )

    extra = {}
    lagged = {}
    for k in range(n):
        inv = leaf_inverse(upper[k, k])
        if k == 0:
            for i in range(n):
                lagged[i] = jnp.concatenate([moment(SIDE, i, j) for j in range(n)], axis=1)
        rest = range(k + 1, n)
        if rest:
            near = dot_nn(inv, upper[k, k + 1])
            left = [near.T]
            upper[k + 1, k + 1] = upper[k + 1, k + 1] - dot_nn(left[0], near)
        others = [upper[k, i] for i in range(k + 2, n)] + ([extra[k]] if k else []) + [lagged[k]]
        others = dot_nn(inv, jnp.concatenate(others, axis=1))
        at = max(n - k - 2, 0) * B
        far = [others[:, i : i + B] for i in range(0, at, B)]
        w_rows = jnp.concatenate([others[:, at : at + k * B], inv], axis=1) if k else inv
        t_rows = others[:, at + k * B :]
        w_ref[k * B : (k + 1) * B, : (k + 1) * B] = w_rows
        wt_ref[: (k + 1) * B, k * B : (k + 1) * B] = w_rows.T
        if k + 1 < n:
            w_ref[k * B : (k + 1) * B, (k + 1) * B :] = jnp.zeros((B, (n - 1 - k) * B), F32)
            wt_ref[(k + 1) * B :, k * B : (k + 1) * B] = jnp.zeros(((n - 1 - k) * B, B), F32)
        t_ref[k * B : (k + 1) * B, :] = t_rows
        if rest:
            left = jnp.concatenate(left + [block.T for block in far], axis=0)
            update = dot_nn(left, jnp.concatenate(far + [w_rows, t_rows], axis=1))
            for i in rest:
                line = update[(i - k - 1) * B : (i - k) * B]
                for j in range(max(i, k + 2), n):
                    upper[i, j] = upper[i, j] - line[:, (j - k - 2) * B : (j - k - 1) * B]
                new = -line[:, at + k * B : at + (k + 1) * B]
                if k:
                    new = jnp.concatenate([extra[i] - line[:, at : at + k * B], new], axis=1)
                extra[i] = new
                lagged[i] = lagged[i] - line[:, at + (k + 1) * B :]
        if k == 0:
            groups = frames // B
            moments = (
                first
                + lax.broadcasted_iota(jnp.int32, (groups, B), 0) * B
                + lax.broadcasted_iota(jnp.int32, (groups, B), 1)
            )
            validity = valid_at(seg_ref, moments)
            first_map = w_ref[comp_rows, :].astype(BF16)
            for low in range(0, frames, step):
                if low + step < frames:
                    ahead = x_ref[low + LAG : low + LAG + step, :B]
                else:
                    ahead = jnp.concatenate(
                        [x_ref[low + LAG : frames, :B], halo_ref[:, :B]], axis=0
                    )
                err_ref[:, low : low + step] = apply(first_map[:, :B], ahead)

    feat_rows = pl.ds(pl.multiple_of(feat * B, B), B)
    lead = jnp.concatenate([t_ref[feat_rows, :], t_ref[comp_rows, :]], axis=0)
    half = width // 2
    low_cols = dot_nn(lead[:, :half], wt_ref[:half, :half])
    koop = jnp.concatenate([low_cols, dot_nn(lead, wt_ref[:, half:])], axis=1)
    koop_ref[...] = koop[:B]
    koop_out = pltpu.make_async_copy(koop_ref, koop_hbm, sems.at[0])
    koop_out.start()
    low_cols = dot_nn(koop[B:], w_ref[:, :half])
    high_cols = dot_nn(koop[B:, half:], w_ref[half:, half:])
    second_map = jnp.concatenate([low_cols, high_cols], axis=1).astype(BF16)
    mean_all = jnp.concatenate(mean_row, axis=1)
    offset = jnp.sum(
        mean_all * (first_map.astype(F32) - second_map.astype(F32)), axis=1, keepdims=True
    )

    parts = 4
    copies = []
    for part in range(parts):
        span = slice(part * frames // parts, (part + 1) * frames // parts)
        for low in range(span.start, span.stop, step):
            backward = apply(second_map, x_ref[low : low + step, :])
            residual = err_ref[:, low : low + step] - backward - offset
            for at in range(step // B):
                g = low // B + at
                keep = jnp.broadcast_to(validity[g : g + 1], (comp_block, B))
                err_ref[:, g * B : (g + 1) * B] = residual[:, at * B : (at + 1) * B] * keep
        copies.append(
            pltpu.make_async_copy(err_ref.at[:, span], err_hbm.at[:, span], sems.at[1 + part])
        )
        copies[part].start()
    koop_out.wait()
    for copy in copies:
        copy.wait()


def swap(shard, *axes):
    last = 2 ** len(axes) - 1
    return lax.ppermute(shard, axes, [(i, last - i) for i in range(last + 1)])


def gather_line(piece):
    count = lax.axis_size("z")
    if count <= 4:
        moved = [
            lax.ppermute(piece, "z", [(i, i ^ m) for i in range(count)]) for m in range(1, count)
        ]
        return jnp.stack([piece] + moved)
    spread = jnp.broadcast_to(piece[None], (count,) + piece.shape)
    order = lax.axis_index("z") ^ jnp.arange(count, dtype=jnp.int32)
    return jnp.take(lax.all_to_all(spread, "z", 0, 0), order, axis=0)


def shards(features, seg_lengths):
    frames, width = features.shape
    line_count = lax.axis_size("z")
    tm_count = line_count * lax.axis_size("x")
    feat_count = lax.axis_size("y") * lax.axis_size("c")
    halo = lax.ppermute(features[:LAG], ("z", "x"), [(i, i - 1) for i in range(1, tm_count)])
    chunk = -(-PACKED // (8 * tm_count)) * 8
    vmem = pl.BlockSpec(memory_space=pltpu.VMEM)
    smem = pl.BlockSpec(memory_space=pltpu.SMEM)
    params = pltpu.CompilerParams(vmem_limit_bytes=VMEM_LIMIT)
    anywhere = pl.BlockSpec(memory_space=pl.ANY)
    partial, tail, total = pl.pallas_call(
        gram_kernel,
        out_shape=[
            jax.ShapeDtypeStruct((2 * PICKED, B), F32),
            jax.ShapeDtypeStruct((LAG, width), BF16),
            jax.ShapeDtypeStruct((8, B), F32),
        ],
        in_specs=[anywhere, anywhere],
        out_specs=[vmem, vmem, vmem],
        scratch_shapes=[
            pltpu.SMEM(seg_lengths.shape, jnp.int32),
            pltpu.VMEM((frames, width), BF16),
            pltpu.VMEM((frames, 3 * B), BF16),
            pltpu.SemaphoreType.DMA((LOADS + 1,)),
        ],
        compiler_params=pltpu.CompilerParams(vmem_limit_bytes=53 * 2**20),
        cost_estimate=pl.CostEstimate(
            flops=2 * frames * 9 * B * B, bytes_accessed=frames * width * 2, transcendentals=0
        ),
        name="grams",
    )(seg_lengths, features)
    partial = pl.pallas_call(
        edge_kernel,
        out_shape=jax.ShapeDtypeStruct((tm_count * chunk, B), F32),
        in_specs=[vmem] * 4,
        out_specs=vmem,
        compiler_params=params,
        name="edges",
    )(partial, tail, total, halo)
    swapped = lax.all_to_all(partial.reshape(tm_count, chunk, B), ("z", "x"), 0, 0)
    summed = jnp.sum(swapped, axis=0)
    line = gather_line(summed)
    held = [line, swap(line, "y"), swap(line, "x"), swap(line, "x", "y")]
    held = held + [swap(part, "c") for part in held]
    return pl.pallas_call(
        solve_kernel,
        out_shape=[
            jax.ShapeDtypeStruct((width // feat_count, width), F32),
            jax.ShapeDtypeStruct((NC // feat_count, frames), F32),
        ],
        in_specs=[smem] + [vmem] * 10,
        out_specs=[anywhere, anywhere],
        scratch_shapes=[
            pltpu.VMEM((width // feat_count, width), F32),
            pltpu.VMEM((NC // feat_count, frames), F32),
            pltpu.VMEM((feat_count, tm_count * chunk, B), F32),
            pltpu.VMEM((width, width), F32),
            pltpu.VMEM((width, width), F32),
            pltpu.VMEM((width, width), F32),
            pltpu.SemaphoreType.DMA((5,)),
        ],
        compiler_params=params,
        name="solve",
    )(seg_lengths, *held, features, halo)


def solution(mesh):
    tm, feat = mesh.shape["tm"], mesh.shape["feat"]
    fine = jax.sharding.Mesh(
        mesh.devices.reshape(tm // 2, 2, feat // 2, 2), ("z", "x", "y", "c")
    )
    in_specs = (P(("z", "x"), None), P())
    out_specs = (P(("y", "c"), None), P(("y", "c"), ("z", "x")))
    return jax.shard_map(shards, mesh=fine, in_specs=in_specs, out_specs=out_specs, check_vma=False)
```

```python
import jax
import jax.numpy as jnp
from jax import lax
from jax.experimental import pallas as pl
from jax.experimental.pallas import tpu as pltpu
from jax.sharding import PartitionSpec as P

LAG = 64
NC = 128
RIDGE = 0.05
HIGHEST = lax.Precision.HIGHEST
B = 128
PICKED = 2 * B + B // 2
SIDE = PICKED - B
PACKED = 2 * SIDE + B + 8
LOADS = 4
AHEAD = 3
F32 = jnp.float32
BF16 = jnp.bfloat16
VMEM_LIMIT = 48 * 2**20


def dot_nn(left, right):
    return jnp.dot(left, right, precision=HIGHEST, preferred_element_type=F32)


def contract(left_rows, right_rows):
    return lax.dot_general(
        left_rows, right_rows, (((0,), (0,)), ((), ())), preferred_element_type=F32
    )


def valid_at(seg_ref, moments):
    def step(k, carry):
        end, crossing = carry
        end = end + seg_ref[k]
        hit = (end > moments) & (end <= moments + LAG)
        return end, jnp.where(hit, 1.0, crossing)

    zero = jnp.zeros(moments.shape, F32)
    _, crossing = lax.fori_loop(0, seg_ref.shape[0], step, (jnp.int32(0), zero), unroll=True)
    return 1.0 - crossing


def own_block(back):
    feat_count = lax.axis_size("y") * lax.axis_size("c")
    feat = lax.axis_index("y") * lax.axis_size("c") + lax.axis_index("c")
    block = lax.rem(feat - back + feat_count, feat_count)
    return pl.ds(pl.multiple_of(block * B, B), B)


def half_block(square):
    feat = lax.axis_index("y") * lax.axis_size("c") + lax.axis_index("c")
    return jnp.where(feat < 2, square.T[: B // 2], square[B // 2 :])


def frame_start(frames):
    return (lax.axis_index("z") * lax.axis_size("x") + lax.axis_index("x")) * frames


def gram_kernel(seg_hbm, x_hbm, out_ref, tail_ref, total_ref, seg_ref, x_ref, z_ref, sems):
    frames = x_ref.shape[0]
    groups = frames // B
    per = frames // LOADS
    lengths = pltpu.make_async_copy(seg_hbm, seg_ref, sems.at[LOADS])
    lengths.start()
    copies = []
    for c in range(LOADS):
        part = pl.ds(c * per, per)
        copies.append(pltpu.make_async_copy(x_hbm.at[part], x_ref.at[part], sems.at[c]))
        copies[c].start()
    first = frame_start(frames)
    cols = own_block(0)
    lengths.wait()
    moments = (
        first
        + lax.broadcasted_iota(jnp.int32, (groups, B), 0) * B
        + lax.broadcasted_iota(jnp.int32, (groups, B), 1)
    )
    ahead = valid_at(seg_ref, moments)
    start = jnp.where(moments[:8] >= LAG, valid_at(seg_ref, moments[:8] - LAG), 0.0)
    columns = jnp.concatenate([ahead, start, jnp.zeros((B - groups - 8, B), F32)], axis=0).T

    def weight(row):
        return jnp.broadcast_to(columns[:, row : row + 1], (B, B))

    weights = [weight(g) for g in range(groups)]
    first_behind = weight(groups)[:LAG]
    total = jnp.zeros((8, B), F32)
    half = B - LAG
    copies[0].wait()
    for c in range(LOADS):
        if c + 1 < LOADS:
            copies[c + 1].wait()
        for g in range(c * per // B, (c + 1) * per // B):
            low = g * B
            own = x_ref[low : low + B, cols].astype(F32)
            if g + 1 < groups:
                later = x_ref[low + LAG : low + LAG + B, cols].astype(F32)
            else:
                later = jnp.concatenate(
                    [x_ref[low + LAG : low + B, cols].astype(F32), jnp.zeros((LAG, B), F32)], axis=0
                )
            if g > 0:
                earlier = x_ref[low - LAG : low - LAG + B, cols].astype(F32)
            else:
                earlier = jnp.concatenate(
                    [jnp.zeros((LAG, B), F32), x_ref[0:half, cols].astype(F32)], axis=0
                )
            before = weights[g - 1][half:] if g > 0 else jnp.zeros((LAG, B), F32)
            behind = jnp.concatenate([before, weights[g][:half]], axis=0)
            both = jnp.concatenate([before if g > 0 else first_behind, weights[g][:half]], axis=0)
            weighted = own * (weights[g] + both)
            z_ref[low : low + B, 0:B] = weighted.astype(BF16)
            z_ref[low : low + B, B : 2 * B] = (later * weights[g]).astype(BF16)
            z_ref[low : low + B, 2 * B : 3 * B] = (earlier * behind).astype(BF16)
            for part in range(B // 8):
                total = total + weighted[8 * part : 8 * part + 8]
    last = x_ref[frames - LAG : frames, :].astype(F32)
    tail_weight = jnp.concatenate([weights[groups - 1][half:]] * (last.shape[1] // B), axis=1)
    tail_ref[...] = (last * tail_weight).astype(BF16)
    total_ref[...] = jnp.broadcast_to(jnp.sum(total, axis=0, keepdims=True), (8, B))
    for back in range(3):
        prod = contract(x_ref[:, own_block(back)], z_ref[...])
        for base, gram in ((0, prod[:, :B]), (PICKED, prod[:, B : 2 * B] + prod[:, 2 * B :])):
            if back < 2:
                out_ref[base + back * B : base + (back + 1) * B, :] = gram
            else:
                out_ref[base + 2 * B : base + PICKED, :] = half_block(gram)


def square_places():
    return lax.broadcasted_iota(jnp.int32, (B, B), 0), lax.broadcasted_iota(jnp.int32, (B, B), 1)


def edge_kernel(part_ref, tail_ref, total_ref, halo_ref, out_ref):
    cols = own_block(0)
    extra = [
        contract(tail_ref[:, own_block(back)], halo_ref[:, cols])
        + contract(halo_ref[:, own_block(back)], tail_ref[:, cols])
        for back in range(3)
    ]
    out_ref[:SIDE, :] = part_ref[B:PICKED, :]
    out_ref[SIDE : SIDE + B, :] = part_ref[PICKED + B : PICKED + 2 * B, :] + extra[1]
    out_ref[SIDE + B : 2 * SIDE, :] = part_ref[PICKED + 2 * B :, :] + half_block(extra[2])
    row, lane = square_places()
    own = part_ref[PICKED : PICKED + B, :] + extra[0]
    out_ref[2 * SIDE : 2 * SIDE + B, :] = jnp.where(lane >= row, part_ref[:B, :], own)
    diag = jnp.sum(jnp.where(lane == row, own, 0.0), axis=0, keepdims=True)
    last = lax.broadcasted_iota(jnp.int32, (8, B), 0)
    last = jnp.where(last == 0, diag, jnp.where(last == 1, total_ref[...], 0.0))
    out_ref[2 * SIDE + B : PACKED, :] = last
    if out_ref.shape[0] > PACKED:
        out_ref[PACKED:, :] = jnp.zeros((out_ref.shape[0] - PACKED, B), F32)


def across(tile, lane):
    return jnp.broadcast_to(tile[:, lane : lane + 1], tile.shape)


def down(tile, row):
    return jnp.broadcast_to(tile[row : row + 1, :], tile.shape)


def leaf_inverse(square):
    count = square.shape[0] // 8
    lanes = lax.broadcasted_iota(jnp.int32, (8, B), 1)
    subs = lax.broadcasted_iota(jnp.int32, (8, B), 0)
    rows = [square[8 * i : 8 * i + 8, :] for i in range(count)]
    result = []
    carried = {}
    for b in range(count):
        block = (lanes >= 8 * b) & (lanes < 8 * b + 8)
        cols = {
            k: carried[k] if k in carried else [across(rows[k], 8 * b + j) for j in range(8)]
            for k in range(b, count)
        }
        direct = range(b + 1, min(count, b + AHEAD + 1))
        coming = {k: [across(rows[k], 8 * b + 8 + j) for j in range(8)] for k in direct}
        rows[b] = jnp.where(block, jnp.where(lanes - 8 * b == subs, 1.0, 0.0), rows[b])
        for k in range(b + 1, count):
            rows[k] = jnp.where(block, 0.0, rows[k])
        panel = cols[b]
        top = rows[b]
        pivots = None
        for i in range(8):
            pivot = down(panel[i], i)
            recip = 1.0 / pivot
            pivots = pivot if pivots is None else jnp.where(subs == i, pivot, pivots)
            factor = jnp.where(subs > i, panel[i] * recip, 0.0)
            line = down(top, i)
            split = [down(panel[i], j) if j > i else None for j in range(8)]
            for j in range(i + 1, 8):
                panel[j] = panel[j] - factor * split[j]
            if i < 7:
                top = top - factor * line
            if direct:
                right = [down(cols[b + 1][i], j) for j in range(8)]
            for k in direct:
                gain = cols[k][i] * recip
                for j in range(8):
                    coming[k][j] = coming[k][j] - gain * right[j]
                for j in range(i + 1, 8):
                    cols[k][j] = cols[k][j] - gain * split[j]
                rows[k] = rows[k] - gain * line
        result.append(jnp.where(lanes < 8 * b + 8, top * lax.rsqrt(pivots), 0.0))
        if b + AHEAD + 1 < count:
            recips = 1.0 / pivots
            solved = top * recips
            for k in range(7, 0, -1):
                back = jnp.where(subs < k, panel[k] * recips, 0.0)
                solved = solved - back * down(solved, k)
            lines = [down(solved, j) for j in range(8)]
            for k in range(b + AHEAD + 1, count):
                p = [cols[k][j] * lines[j] for j in range(8)]
                rows[k] = rows[k] - (((p[0] + p[1]) + (p[2] + p[3])) + ((p[4] + p[5]) + (p[6] + p[7])))
        carried = coming
    return jnp.concatenate(result, axis=0)


def solve_kernel(seg_ref, *refs):
    sums_refs, (x_ref, halo_ref, koop_hbm, err_hbm) = refs[:8], refs[8:12]
    koop_ref, err_ref, flat_ref, w_ref, wt_ref, t_ref, sems = refs[12:]
    frames, width = x_ref.shape
    n = feat_count = width // B
    lines, chunk = sums_refs[0].shape[:2]
    first = frame_start(frames)
    z, x, y, c = [lax.axis_index(name) for name in ("z", "x", "y", "c")]
    feat = y * 2 + c
    for at, sums_ref in enumerate(sums_refs):
        flip_c, flip_x, flip_y = at // 4, (at // 2) % 2, at % 2
        source = (y ^ flip_y) * 2 + (c ^ flip_c)
        for line in range(lines):
            low = pl.multiple_of(((z ^ line) * 2 + (x ^ flip_x)) * chunk, 8)
            flat_ref[source, pl.ds(low, chunk), :] = sums_ref[line]

    def add_pairs(k, total):
        return total + jnp.maximum(seg_ref[k] - LAG, 0)

    pairs = lax.fori_loop(0, seg_ref.shape[0], add_pairs, jnp.int32(0), unroll=True)
    ones = jnp.ones((8, B), F32)
    inv_pairs = (1.0 / (ones * (2.0 * pairs.astype(F32))))[0:1, :]
    row, lane = square_places()
    low = 2 * SIDE + B
    mean_row = [flat_ref[f, low + 1 : low + 2, :] * inv_pairs for f in range(n)]
    mean_col = [jnp.broadcast_to(mean_row[f], (B, B)).T for f in range(n)]

    squares = [flat_ref[f, 2 * SIDE : 2 * SIDE + B, :] for f in range(n)]
    turned = [square.T for square in squares]

    def summed(base, i, j):
        back = (j - i) % n
        if back == 0 and base == 0:
            return jnp.where(lane >= row, squares[i], turned[i])
        if back == 0:
            diag = jnp.broadcast_to(flat_ref[i, 2 * SIDE + B : 2 * SIDE + B + 1, :], (B, B))
            return jnp.where(lane == row, diag, jnp.where(lane < row, squares[i], turned[i]))
        if back == 1:
            return flat_ref[j, base : base + B, :]
        if i < j and back == 2:
            pieces = [flat_ref[f, base + B : base + SIDE, :] for f in (i, j)]
            return jnp.concatenate(pieces, axis=0)
        return summed(base, j, i).T

    def moment(base, i, j):
        return summed(base, i, j) * inv_pairs - mean_col[i] * mean_row[j]

    eye = row == lane
    upper = {(i, j): moment(0, i, j) for i in range(n) for j in range(i, n)}
    diag_sum = sum(jnp.where(eye, upper[i, i], 0.0) for i in range(n))
    trace = jnp.sum(jnp.sum(diag_sum, axis=0, keepdims=True), axis=1, keepdims=True)
    ridge = jnp.where(eye, jnp.broadcast_to(RIDGE * (trace / width), (B, B)), 0.0)
    for i in range(n):
        upper[i, i] = upper[i, i] + ridge
    comp_block = NC // feat_count
    comp_rows = pl.ds(pl.multiple_of(feat * comp_block, comp_block), comp_block)
    step = 2 * B

    def apply(maps, frames_block):
        return lax.dot_general(
            maps, frames_block, (((1,), (1,)), ((), ())), preferred_element_type=F32
        )

    extra = {}
    lagged = {}
    for k in range(n):
        inv = leaf_inverse(upper[k, k])
        if k == 0:
            for i in range(n):
                lagged[i] = jnp.concatenate([moment(SIDE, i, j) for j in range(n)], axis=1)
        rest = range(k + 1, n)
        if rest:
            near = dot_nn(inv, upper[k, k + 1])
            left = [near.T]
            upper[k + 1, k + 1] = upper[k + 1, k + 1] - dot_nn(left[0], near)
        others = [upper[k, i] for i in range(k + 2, n)] + ([extra[k]] if k else []) + [lagged[k]]
        others = dot_nn(inv, jnp.concatenate(others, axis=1))
        at = max(n - k - 2, 0) * B
        far = [others[:, i : i + B] for i in range(0, at, B)]
        w_rows = jnp.concatenate([others[:, at : at + k * B], inv], axis=1) if k else inv
        t_rows = others[:, at + k * B :]
        w_ref[k * B : (k + 1) * B, : (k + 1) * B] = w_rows
        wt_ref[: (k + 1) * B, k * B : (k + 1) * B] = w_rows.T
        if k + 1 < n:
            w_ref[k * B : (k + 1) * B, (k + 1) * B :] = jnp.zeros((B, (n - 1 - k) * B), F32)
            wt_ref[(k + 1) * B :, k * B : (k + 1) * B] = jnp.zeros(((n - 1 - k) * B, B), F32)
        t_ref[k * B : (k + 1) * B, :] = t_rows
        if rest:
            left = jnp.concatenate(left + [block.T for block in far], axis=0)
            update = dot_nn(left, jnp.concatenate(far + [w_rows, t_rows], axis=1))
            for i in rest:
                line = update[(i - k - 1) * B : (i - k) * B]
                for j in range(max(i, k + 2), n):
                    upper[i, j] = upper[i, j] - line[:, (j - k - 2) * B : (j - k - 1) * B]
                new = -line[:, at + k * B : at + (k + 1) * B]
                if k:
                    new = jnp.concatenate([extra[i] - line[:, at : at + k * B], new], axis=1)
                extra[i] = new
                lagged[i] = lagged[i] - line[:, at + (k + 1) * B :]
        if k == 0:
            groups = frames // B
            moments = (
                first
                + lax.broadcasted_iota(jnp.int32, (groups, B), 0) * B
                + lax.broadcasted_iota(jnp.int32, (groups, B), 1)
            )
            validity = valid_at(seg_ref, moments)
            first_map = w_ref[comp_rows, :].astype(BF16)
            for low in range(0, frames, step):
                if low + step < frames:
                    ahead = x_ref[low + LAG : low + LAG + step, :B]
                else:
                    ahead = jnp.concatenate(
                        [x_ref[low + LAG : frames, :B], halo_ref[:, :B]], axis=0
                    )
                err_ref[:, low : low + step] = apply(first_map[:, :B], ahead)

    feat_rows = pl.ds(pl.multiple_of(feat * B, B), B)
    lead = jnp.concatenate([t_ref[feat_rows, :], t_ref[comp_rows, :]], axis=0)
    half = width // 2
    low_cols = dot_nn(lead[:, :half], wt_ref[:half, :half])
    koop = jnp.concatenate([low_cols, dot_nn(lead, wt_ref[:, half:])], axis=1)
    koop_ref[...] = koop[:B]
    koop_out = pltpu.make_async_copy(koop_ref, koop_hbm, sems.at[0])
    koop_out.start()
    low_cols = dot_nn(koop[B:], w_ref[:, :half])
    high_cols = dot_nn(koop[B:, half:], w_ref[half:, half:])
    second_map = jnp.concatenate([low_cols, high_cols], axis=1).astype(BF16)
    mean_all = jnp.concatenate(mean_row, axis=1)
    offset = jnp.sum(
        mean_all * (first_map.astype(F32) - second_map.astype(F32)), axis=1, keepdims=True
    )

    parts = 4
    copies = []
    for part in range(parts):
        span = slice(part * frames // parts, (part + 1) * frames // parts)
        for low in range(span.start, span.stop, step):
            backward = apply(second_map, x_ref[low : low + step, :])
            residual = err_ref[:, low : low + step] - backward - offset
            for at in range(step // B):
                g = low // B + at
                keep = jnp.broadcast_to(validity[g : g + 1], (comp_block, B))
                err_ref[:, g * B : (g + 1) * B] = residual[:, at * B : (at + 1) * B] * keep
        copies.append(
            pltpu.make_async_copy(err_ref.at[:, span], err_hbm.at[:, span], sems.at[1 + part])
        )
        copies[part].start()
    koop_out.wait()
    for copy in copies:
        copy.wait()


def swap(shard, *axes):
    last = 2 ** len(axes) - 1
    return lax.ppermute(shard, axes, [(i, last - i) for i in range(last + 1)])


def gather_line(piece):
    count = lax.axis_size("z")
    if count <= 4:
        moved = [
            lax.ppermute(piece, "z", [(i, i ^ m) for i in range(count)]) for m in range(1, count)
        ]
        return jnp.stack([piece] + moved)
    spread = jnp.broadcast_to(piece[None], (count,) + piece.shape)
    order = lax.axis_index("z") ^ jnp.arange(count, dtype=jnp.int32)
    return jnp.take(lax.all_to_all(spread, "z", 0, 0), order, axis=0)


def shards(features, seg_lengths):
    frames, width = features.shape
    line_count = lax.axis_size("z")
    tm_count = line_count * lax.axis_size("x")
    feat_count = lax.axis_size("y") * lax.axis_size("c")
    halo = lax.ppermute(features[:LAG], ("z", "x"), [(i, i - 1) for i in range(1, tm_count)])
    chunk = -(-PACKED // (8 * tm_count)) * 8
    vmem = pl.BlockSpec(memory_space=pltpu.VMEM)
    smem = pl.BlockSpec(memory_space=pltpu.SMEM)
    params = pltpu.CompilerParams(vmem_limit_bytes=VMEM_LIMIT)
    anywhere = pl.BlockSpec(memory_space=pl.ANY)
    partial, tail, total = pl.pallas_call(
        gram_kernel,
        out_shape=[
            jax.ShapeDtypeStruct((2 * PICKED, B), F32),
            jax.ShapeDtypeStruct((LAG, width), BF16),
            jax.ShapeDtypeStruct((8, B), F32),
        ],
        in_specs=[anywhere, anywhere],
        out_specs=[vmem, vmem, vmem],
        scratch_shapes=[
            pltpu.SMEM(seg_lengths.shape, jnp.int32),
            pltpu.VMEM((frames, width), BF16),
            pltpu.VMEM((frames, 3 * B), BF16),
            pltpu.SemaphoreType.DMA((LOADS + 1,)),
        ],
        compiler_params=pltpu.CompilerParams(vmem_limit_bytes=53 * 2**20),
        cost_estimate=pl.CostEstimate(
            flops=2 * frames * 9 * B * B, bytes_accessed=frames * width * 2, transcendentals=0
        ),
        name="grams",
    )(seg_lengths, features)
    partial = pl.pallas_call(
        edge_kernel,
        out_shape=jax.ShapeDtypeStruct((tm_count * chunk, B), F32),
        in_specs=[vmem] * 4,
        out_specs=vmem,
        compiler_params=params,
        name="edges",
    )(partial, tail, total, halo)
    swapped = lax.all_to_all(partial.reshape(tm_count, chunk, B), ("z", "x"), 0, 0)
    summed = jnp.sum(swapped, axis=0)
    line = gather_line(summed)
    held = [line, swap(line, "y"), swap(line, "x"), swap(line, "x", "y")]
    held = held + [swap(part, "c") for part in held]
    return pl.pallas_call(
        solve_kernel,
        out_shape=[
            jax.ShapeDtypeStruct((width // feat_count, width), F32),
            jax.ShapeDtypeStruct((NC // feat_count, frames), F32),
        ],
        in_specs=[smem] + [vmem] * 10,
        out_specs=[anywhere, anywhere],
        scratch_shapes=[
            pltpu.VMEM((width // feat_count, width), F32),
            pltpu.VMEM((NC // feat_count, frames), F32),
            pltpu.VMEM((feat_count, tm_count * chunk, B), F32),
            pltpu.VMEM((width, width), F32),
            pltpu.VMEM((width, width), F32),
            pltpu.VMEM((width, width), F32),
            pltpu.SemaphoreType.DMA((5,)),
        ],
        compiler_params=params,
        name="solve",
    )(seg_lengths, *held, features, halo)


def solution(mesh):
    tm, feat = mesh.shape["tm"], mesh.shape["feat"]
    fine = jax.sharding.Mesh(
        mesh.devices.reshape(tm // 2, 2, feat // 2, 2), ("z", "x", "y", "c")
    )
    in_specs = (P(("z", "x"), None), P())
    out_specs = (P(("y", "c"), None), P(("y", "c"), ("z", "x")))
    return jax.shard_map(shards, mesh=fine, in_specs=in_specs, out_specs=out_specs, check_vma=False)
```
